256 devices in a mesh: seq: 128 (over x, y, z), head: 2 (over core).
Axes of the slice: x: 4, y: 4, z: 8, core: 2. Of those that a mesh axis runs over, the one named last changes fastest.
Arguments:
- tokens: bfloat16 [65536, 1024], P('seq', 'head'), may hold values from -16 to 16
- w_qk: bfloat16 [1024, 2, 1024], P(None, None, 'head'), may hold values from -0.1875 to 0.1875
- w_value: bfloat16 [1024, 1024], P(None, 'head'), may hold values from -0.75 to 0.75
- span_start: int32 [512], P('seq'), may hold values from 0 to 65408, as said below
- span_end: int32 [512], P('seq'), may hold values from 128 to 65536, as said below
Outputs:
- attended: bfloat16 [65536, 1024], P('seq', 'head')
The draws below stay inside these ranges and needn't reach their ends.
Inputs may be any that keep to these rules, and one draw needn't show every extreme that they name: span_start[b] is at least (b - 1) * 128 and at most b * 128, never below 0; the last block's span starts at its own first token. span_end[b] is at least (b + 1) * 128 and at most (b + 2) * 128, never above 65536; the first block's span ends at its own last token plus one.
All inputs are finite; a program needn't handle non-finite values.
Results may differ from the reference program's by a relative error of at most 0.0029.
The reference program's roundings to bfloat16 on the way count: a program that leaves them out, or rounds other values in their place, can miss the bound.
Values may be sent and summed in bfloat16 or wider, within the bound.
A program may use at most 64 MiB of HBM per device.

```python
import math
import jax
import jax.numpy as jnp
from jax import lax

D = 1024
HEADS = 8
HD = 128
B = 128
LEVELS = 6
TOKENS = 65536
NBLK = 512


def draw_tokens(key, part):
    key = jax.random.fold_in(key, 11)
    region_key, noise_key = jax.random.split(key, 2)
    regions = jax.random.normal(region_key, (TOKENS // 64, D), jnp.float32)
    shared = jnp.repeat(regions, 64, axis=0)
    values = jax.random.normal(noise_key, (TOKENS, D), jnp.float32) + 0.7 * shared
    return jnp.clip(values, -16.0, 16.0).astype(jnp.bfloat16)


def draw_span_start(key, part):
    key = jax.random.fold_in(key, 21)
    reach = jax.random.randint(key, (NBLK,), 0, B + 1, dtype=jnp.int32)
    block_ids = jnp.arange(NBLK, dtype=jnp.int32)
    reach = jnp.where(block_ids == NBLK - 1, 0, reach)
    return jnp.maximum(0, block_ids * B - reach).astype(jnp.int32)


def draw_span_end(key, part):
    key = jax.random.fold_in(key, 22)
    reach = jax.random.randint(key, (NBLK,), 0, B + 1, dtype=jnp.int32)
    block_ids = jnp.arange(NBLK, dtype=jnp.int32)
    reach = jnp.where(block_ids == 0, 0, reach)
    return jnp.minimum(TOKENS, (block_ids + 1) * B + reach).astype(jnp.int32)


def shard_levels(rng, dims, cuts, smallest, largest):
    gain, own = 1.0, jax.random.fold_in(rng, 6)
    for dim, parts in cuts:
        draws = jnp.exp(jax.random.uniform(jax.random.fold_in(own, dim), (parts,), jnp.float32, smallest / len(cuts), largest / len(cuts)))
        gain = gain * jnp.repeat(draws, dims[dim] // parts).reshape([-1 if axis == dim else 1 for axis in range(len(dims))])
    return gain


def normal_values(key, shape, width, limit, pieces=(), kind=jnp.bfloat16):
    level = shard_levels(key, shape, pieces, -0.22, 0.18) if pieces else 1.0
    result = jax.random.normal(key, shape, jnp.float32) * width * level
    return jnp.minimum(jnp.maximum(result, -limit), limit).astype(kind)


def setup_inputs(seed: int = 0) -> dict:
    arg_keys = jax.random.split(jax.random.key(seed), 6)
    return {
        "tokens": draw_tokens(jax.random.fold_in(arg_keys[5], 71), 0),
        "w_qk": normal_values(arg_keys[1], (D, 2, HEADS * HD), D ** -0.5, 0.1875, ((2, 2),)),
        "w_value": normal_values(arg_keys[2], (D, HEADS * HD), (D // 16) ** -0.5, 0.75, ((1, 2),)),
        "span_start": draw_span_start(jax.random.fold_in(arg_keys[5], 71), 0),
        "span_end": draw_span_end(jax.random.fold_in(arg_keys[5], 71), 0),
    }


def pool_rows(values):
    wide = values.astype(jnp.float32)
    paired = wide.reshape((wide.shape[0] // 2, 2) + wide.shape[1:])
    return ((paired[:, 0] + paired[:, 1]) * 0.5).astype(jnp.bfloat16)

def merge_state(state, update):
    peak, total, numerator = state
    peak_new, total_new, numer_new = update
    highest = jnp.maximum(peak, peak_new)
    keep_old = jnp.exp(peak - highest)
    keep_new = jnp.exp(peak_new - highest)
    total = total * keep_old + total_new * keep_new
    numerator = numerator * keep_old[..., None] + numer_new * keep_new[..., None]
    return (highest, total, numerator)

def fine_level(query, keys, values, span_start, span_end):
    scale = 1.0 / math.sqrt(HD)
    zero_rim = jnp.zeros((B, HEADS * HD), jnp.bfloat16)
    keys_pad = jnp.concatenate([zero_rim, keys, zero_rim], axis=0)
    values_pad = jnp.concatenate([zero_rim, values, zero_rim], axis=0)

    def one_block(block_id):
        start_row = block_id * B
        query_rows = lax.dynamic_slice_in_dim(query, start_row, B, 0).reshape(B, HEADS, HD).astype(jnp.float32)
        key_rows = lax.dynamic_slice_in_dim(keys_pad, start_row, 3 * B, 0).reshape(3 * B, HEADS, HD).astype(jnp.float32)
        value_rows = lax.dynamic_slice_in_dim(values_pad, start_row, 3 * B, 0).reshape(3 * B, HEADS, HD).astype(jnp.float32)
        scores = jnp.einsum('ihd,jhd->hij', query_rows, key_rows) * scale
        position = (block_id - 1) * B + jnp.arange(3 * B, dtype=jnp.int32)
        inside = (position >= span_start[block_id]) & (position < span_end[block_id])
        scores = jnp.where(inside[None, None, :], scores, -jnp.inf)
        peak = lax.optimization_barrier(jnp.max(scores, axis=-1))
        weights = jnp.exp(scores - peak[..., None])
        total = lax.optimization_barrier(jnp.sum(weights, axis=-1))
        numerator = jnp.einsum('hij,jhd->ihd', weights.astype(jnp.bfloat16).astype(jnp.float32), value_rows)
        return (peak.T, total.T, numerator)
    peak, total, numerator = lax.map(one_block, jnp.arange(NBLK, dtype=jnp.int32))
    return (peak.reshape(TOKENS, HEADS), total.reshape(TOKENS, HEADS), numerator.reshape(TOKENS, HEADS, HD))

def coarse_level(query_level, keys_level, values_level, level):
    scale = 1.0 / math.sqrt(HD)
    rows = query_level.shape[0]
    count = rows // B
    query_blocks = query_level.reshape(count, B, HEADS, HD).astype(jnp.float32)
    key_blocks = jnp.flip(keys_level.reshape(count // 2, 2, B, HEADS, HD), axis=1).reshape(count, B, HEADS, HD).astype(jnp.float32)
    value_blocks = jnp.flip(values_level.reshape(count // 2, 2, B, HEADS, HD), axis=1).reshape(count, B, HEADS, HD).astype(jnp.float32)
    scores = jnp.einsum('cihd,cjhd->chij', query_blocks, key_blocks) * scale
    peak = lax.optimization_barrier(jnp.max(scores, axis=-1))
    weights = jnp.exp(scores - peak[..., None])
    total = lax.optimization_barrier(jnp.sum(weights, axis=-1))
    numerator = jnp.einsum('chij,cjhd->cihd', weights.astype(jnp.bfloat16).astype(jnp.float32), value_blocks)
    peak = jnp.transpose(peak, (0, 2, 1)).reshape(rows, HEADS)
    total = jnp.transpose(total, (0, 2, 1)).reshape(rows, HEADS)
    numerator = numerator.reshape(rows, HEADS, HD)
    factor = 2 ** level
    return (jnp.repeat(peak, factor, axis=0), jnp.repeat(total, factor, axis=0), jnp.repeat(numerator, factor, axis=0))

def reference(tokens, w_qk, w_value, span_start, span_end):
    query = jnp.dot(tokens, w_qk[:, 0, :], preferred_element_type=jnp.float32).astype(jnp.bfloat16)
    keys = jnp.dot(tokens, w_qk[:, 1, :], preferred_element_type=jnp.float32).astype(jnp.bfloat16)
    values = jnp.dot(tokens, w_value, preferred_element_type=jnp.float32).astype(jnp.bfloat16)
    state = fine_level(query, keys, values, span_start, span_end)
    query_level, keys_level, values_level = (query, keys, values)
    for level in range(1, LEVELS + 1):
        query_level = pool_rows(query_level)
        keys_level = pool_rows(keys_level)
        values_level = pool_rows(values_level)
        state = merge_state(state, coarse_level(query_level, keys_level, values_level, level))
    peak, total, numerator = state
    return (numerator / total[..., None]).astype(jnp.bfloat16).reshape(TOKENS, HEADS * HD)
```

```python
import functools
import math

import jax
import jax.numpy as jnp
from jax import lax
from jax.experimental import pallas as pl
from jax.experimental.pallas import tpu as pltpu
from jax.sharding import PartitionSpec as P

HD = 128
B = 128
LEVELS = 6
MESH = pl.DeviceIdType.MESH
BF = jnp.bfloat16
F32 = jnp.float32
UNIT = math.log2(math.e) / math.sqrt(HD)


def reversed_bits(x, bits=7):
    out = jnp.zeros_like(x)
    for i in range(bits):
        out = out + (((x >> i) & 1) << (bits - 1 - i))
    return out


def dot(a, b):
    return jnp.dot(a, b, preferred_element_type=F32)


def pool_halves(x, blocks):
    rows, cols = x.shape
    y = x.reshape(blocks, 2, rows // (2 * blocks), cols)
    y = (y[:, 0] + y[:, 1]) * 0.5
    return y.reshape(rows // 2, cols).astype(BF)


def twice(x, blocks):
    rows, cols = x.shape
    y = x.reshape(blocks, rows // blocks, cols)
    return jnp.concatenate([y, y], axis=1).reshape(2 * rows, cols)


def attend(q, k, v, bias=None):
    s = lax.dot_general(q, k, (((1,), (1,)), ((), ())), preferred_element_type=F32)
    if bias is not None:
        s = s + bias
    top = jnp.max(s, axis=-1, keepdims=True)
    w = jnp.exp2((s - top) * UNIT)
    return top * UNIT, jnp.sum(w, axis=-1, keepdims=True), dot(w.astype(BF), v)


def merge(a, b):
    top = jnp.maximum(a[0], b[0])
    ka, kb = jnp.exp2(a[0] - top), jnp.exp2(b[0] - top)
    return top, a[1] * ka + b[1] * kb, a[2] * ka + b[2] * kb


def group(level):
    return 1 << (level - 2)


def siblings(me, level):
    g = group(level)
    own = me // g
    base = (own + 1 - 2 * (own % 2)) * g
    return [base + (me + k) % g for k in range(g)]


def kernel(
    count,
    tok_hbm, wqk_hbm, wv_hbm, start_ref, end_ref,
    out_ref,
    tok_raw, tokp, wqk, wv, wq_s, wk_s, acc,
    q0, k0, v0, q1, k1, v1, q2, q3, q4, q5, q6,
    s2, s3, s4, s5, s6,
    r2, r3, r4, r5, r6,
    fpeak, ftot, fnum,
    load_sem, send_sem, recv_sem,
):
    me, core = lax.axis_index("seq"), lax.axis_index("head")
    heads = q0.shape[0]
    sends = {2: s2, 3: s3, 4: s4, 5: s5, 6: s6}
    lands = {2: r2, 3: r3, 4: r4, 5: r5, 6: r6}

    loads = [
        pltpu.make_async_copy(tok_hbm, tok_raw, load_sem.at[0]),
        pltpu.make_async_copy(wqk_hbm, wqk, load_sem.at[1]),
        pltpu.make_async_copy(wv_hbm, wv, load_sem.at[2]),
    ]
    for load in loads:
        load.start()

    right, left = (me + 1) % count, (me + count - 1) % count
    twin = (me, 1 - core)
    greet = [twin, (right, core), (left, core)]
    for level in range(2, LEVELS + 1):
        greet += [(p, core) for p in siblings(me, level)]
    barrier = pltpu.get_barrier_semaphore()
    for device in greet:
        pl.semaphore_signal(barrier, inc=1, device_id=device, device_id_type=MESH)

    row = lax.broadcasted_iota(jnp.int32, (B, B), 0)
    col = lax.broadcasted_iota(jnp.int32, (B, B), 1)
    perm = jnp.where(reversed_bits(row) == col, 1.0, 0.0).astype(BF)

    loads[0].wait()
    for b in range(4):
        tokp[core, b + 1] = dot(perm, tok_raw[b * B : (b + 1) * B]).astype(BF)

    pl.semaphore_wait(barrier, len(greet))

    def send(src, dst, sem, device):
        copy = pltpu.make_async_remote_copy(
            src_ref=src, dst_ref=dst, send_sem=send_sem.at[sem], recv_sem=recv_sem.at[sem],
            device_id=device, device_id_type=MESH,
        )
        copy.start()
        return copy

    swap = send(tokp.at[core, pl.ds(1, 4)], tokp.at[core, pl.ds(1, 4)], 0, twin)
    to_right = send(tokp.at[core, 4], tokp.at[core, 0], 1, (right, core))
    to_left = send(tokp.at[core, 1], tokp.at[core, 5], 7, (left, core))

    loads[1].wait()
    wq_s[...] = wqk[:, 0, :]
    wk_s[...] = wqk[:, 1, :]
    loads[2].wait()

    half = pl.multiple_of(core * 512, 512)
    other = pl.multiple_of((1 - core) * 512, 512)
    weights = (wk_s, wv, wq_s)
    mine = tokp[core, 1:5].reshape(4 * B, 512)
    for i, w in enumerate(weights):
        acc[i] = dot(mine, w[pl.ds(half, 512), :])

    swap.wait()
    theirs = tokp[1 - core, 1:5].reshape(4 * B, 512)

    quarter_row = lax.broadcasted_iota(jnp.int32, (32, 32), 0)
    quarter_col = lax.broadcasted_iota(jnp.int32, (32, 32), 1)

    def mix(rows, apart):
        r, c = quarter_row[:rows], quarter_col[:rows]
        return jnp.where((c == r) | (c == (r ^ apart)), 0.5, 0.0).astype(BF)

    def narrow():
        r = lax.broadcasted_iota(jnp.int32, (16, 32), 0)
        c = lax.broadcasted_iota(jnp.int32, (16, 32), 1)
        first = (r // 4) * 8 + r % 4
        five = jnp.where((c == first) | (c == first + 4), 0.5, 0.0).astype(BF)
        r = lax.broadcasted_iota(jnp.int32, (8, 16), 0)
        c = lax.broadcasted_iota(jnp.int32, (8, 16), 1)
        first = (r // 2) * 4 + r % 2
        six = jnp.where((c == first) | (c == first + 2), 0.5, 0.0).astype(BF)
        return five, six

    five, six = narrow()
    last = {}
    for i in range(2):
        full = (acc[i] + dot(theirs, weights[i][pl.ds(other, 512), :])).astype(BF)
        x = full.astype(F32)
        store0, store1 = (k0, k1) if i == 0 else (v0, v1)
        for h in range(heads):
            cols = slice(h * HD, (h + 1) * HD)
            store0[h, B : 5 * B] = full[:, cols]
        l1 = pool_halves(x, 4)
        l2 = pool_halves(l1.astype(F32), 4)
        l3 = pool_halves(l2.astype(F32), 4)
        l4 = pool_halves(l3.astype(F32), 4)
        l5 = dot(five, l4).astype(BF)
        l6 = dot(six, l5)
        for h in range(heads):
            cols = slice(h * HD, (h + 1) * HD)
            store1[h] = l1[:, cols]
            s2[h, i] = l2[:, cols]
            s3[h, i] = l3[:, cols]
            s4[h, i] = l4[:, cols]
            s5[h, i] = l5[:, cols]
        last[i] = l6
    both = jnp.concatenate([last[0], last[1]], axis=0).astype(BF)
    for h in range(heads):
        s6[h] = both[:, h * HD : (h + 1) * HD]

    send(s2, r2, 2, (siblings(me, 2)[0], core))
    for level in range(3, LEVELS + 1):
        for p in siblings(me, level):
            send(sends[level], lands[level].at[me % group(level)], level, (p, core))

    full = (acc[2] + dot(theirs, wq_s[pl.ds(other, 512), :])).astype(BF)
    l1 = pool_halves(full.astype(F32), 4)
    l2 = pool_halves(l1.astype(F32), 4)
    l3 = pool_halves(l2.astype(F32), 4)
    l4 = pool_halves(l3.astype(F32), 4)
    l5 = dot(mix(32, 4), l4).astype(BF)
    l6 = dot(mix(32, 2), l5).astype(BF)
    for h in range(heads):
        cols = slice(h * HD, (h + 1) * HD)
        q0[h] = full[:, cols]
        q1[h] = l1[:, cols]
        q2[h] = l2[:, cols]
        q3[h] = l3[:, cols]
        q4[h] = l4[:, cols]
        q5[h] = l5[:, cols]
        q6[h] = l6[:, cols]

    to_right.wait_recv()
    relay_left = send(tokp.at[core, 0], tokp.at[core, 0], 8, twin)
    to_left.wait_recv()
    relay_right = send(tokp.at[core, 5], tokp.at[core, 5], 9, twin)
    relay_left.wait_recv()
    relay_right.wait_recv()

    for store, w in ((k0, wk_s), (v0, wv)):
        for b in (0, 5):
            full = dot(tokp[core, b], w[pl.ds(half, 512), :]) + dot(
                tokp[1 - core, b], w[pl.ds(other, 512), :]
            )
            full = full.astype(BF)
            for h in range(heads):
                store[h, b * B : (b + 1) * B] = full[:, h * HD : (h + 1) * HD]

    place = reversed_bits(lax.broadcasted_iota(jnp.int32, (1, B), 1))
    none = jnp.zeros((1, B), F32)
    biases = []
    for b in range(4):
        before = (me * 4 + b - 1) * B + place
        after = (me * 4 + b + 1) * B + place
        biases.append(
            jnp.concatenate(
                [
                    jnp.where(before >= start_ref[b], 0.0, -jnp.inf),
                    none,
                    jnp.where(after < end_ref[b], 0.0, -jnp.inf),
                ],
                axis=1,
            )
        )

    def near(h, carry):
        for b in range(4):
            c = b // 2
            o = (c ^ 1) * B
            rows = slice(b * B, (b + 1) * B)
            fine = attend(q0[h, rows], k0[h, b * B : (b + 3) * B], v0[h, b * B : (b + 3) * B], biases[b])
            coarse = attend(q1[h, b * 64 : (b + 1) * 64], k1[h, o : o + B], v1[h, o : o + B])
            state = merge(fine, tuple(twice(x, 1) for x in coarse))
            fpeak[h, rows], ftot[h, rows], fnum[h, rows] = state
        return carry

    lax.fori_loop(0, heads, near, 0)

    def landed(level):
        n = lands[level]
        pltpu.make_async_copy(n, n, recv_sem.at[level]).wait()

    for level in range(LEVELS, 1, -1):
        landed(level)

    def far(h, carry):
        k6 = r6[:, h].astype(F32).reshape(16, 2, 8, HD)
        six = attend(q6[h], k6[:, 0].reshape(B, HD).astype(BF), k6[:, 1].reshape(B, HD).astype(BF))
        state = merge(attend(q5[h], r5[:, h, 0].reshape(B, HD), r5[:, h, 1].reshape(B, HD)), six)
        state = merge(attend(q4[h], r4[:, h, 0].reshape(B, HD), r4[:, h, 1].reshape(B, HD)), state)
        state = tuple(twice(x, 4) for x in state)
        state = merge(attend(q3[h], r3[:, h, 0].reshape(B, HD), r3[:, h, 1].reshape(B, HD)), state)
        state = tuple(twice(x, 4) for x in state)
        state = merge(attend(q2[h], r2[h, 0], r2[h, 1]), state)
        cols = pl.ds(pl.multiple_of(h * HD, HD), HD)
        for b in range(4):
            rows = slice(b * B, (b + 1) * B)
            part = tuple(twice(twice(x[b * 32 : (b + 1) * 32], 1), 1) for x in state)
            peak, total, numer = merge((fpeak[h, rows], ftot[h, rows], fnum[h, rows]), part)
            out_ref[rows, cols] = dot(perm, (numer / total).astype(BF)).astype(BF)
        return carry

    lax.fori_loop(0, heads, far, 0)

    to_right.wait_send()
    to_left.wait_send()
    relay_left.wait_send()
    relay_right.wait_send()
    for level in range(2, LEVELS + 1):
        n = lands[level]
        pltpu.make_async_copy(n, n, send_sem.at[level]).wait()


def on_device(count, tokens, w_qk, w_value, span_start, span_end):
    rows, feats = tokens.shape
    heads = w_value.shape[1] // HD
    anywhere = pl.BlockSpec(memory_space=pl.ANY)
    scalar = pl.BlockSpec(memory_space=pltpu.SMEM)

    def vm(*shape, dtype=BF):
        return pltpu.VMEM(shape, dtype)

    width = heads * HD
    scratch = [
        vm(rows, feats), vm(2, 6, B, feats), vm(2 * feats, 2, width), vm(2 * feats, width),
        vm(2 * feats, width), vm(2 * feats, width), vm(3, rows, width, dtype=F32),
        vm(heads, rows, HD), vm(heads, rows + 2 * B, HD), vm(heads, rows + 2 * B, HD),
        vm(heads, 256, HD), vm(heads, 256, HD), vm(heads, 256, HD),
        vm(heads, 128, HD), vm(heads, 64, HD), vm(heads, 32, HD), vm(heads, 32, HD), vm(heads, 32, HD),
        vm(heads, 2, 128, HD), vm(heads, 2, 64, HD), vm(heads, 2, 32, HD), vm(heads, 2, 16, HD), vm(heads, 16, HD),
        vm(heads, 2, 128, HD), vm(2, heads, 2, 64, HD), vm(4, heads, 2, 32, HD), vm(8, heads, 2, 16, HD), vm(16, heads, 16, HD),
        vm(heads, rows, 1, dtype=F32), vm(heads, rows, 1, dtype=F32), vm(heads, rows, HD, dtype=F32),
        pltpu.SemaphoreType.DMA((3,)), pltpu.SemaphoreType.DMA((10,)), pltpu.SemaphoreType.DMA((10,)),
    ]
    return pl.pallas_call(
        functools.partial(kernel, count),
        out_shape=jax.ShapeDtypeStruct((rows, width), BF),
        in_specs=[anywhere, anywhere, anywhere, scalar, scalar],
        out_specs=pl.BlockSpec(memory_space=pltpu.VMEM),
        scratch_shapes=scratch,
        name="htransformer",
        cost_estimate=pl.CostEstimate(flops=3 * 10**9, bytes_accessed=5 * 10**6, transcendentals=10**6),
        compiler_params=pltpu.CompilerParams(
            collective_id=0, has_side_effects=True, vmem_limit_bytes=48 * 2**20
        ),
    )(tokens, w_qk, w_value, span_start, span_end)


def solution(mesh):
    placed = (P("seq", "head"), P(None, None, "head"), P(None, "head"), P("seq"), P("seq"))
    return jax.shard_map(
        functools.partial(on_device, mesh.shape["seq"]),
        mesh=mesh, in_specs=placed, out_specs=P("seq", "head"), check_vma=False,
    )
```

```python
import functools
import math

import jax
import jax.numpy as jnp
from jax import lax
from jax.experimental import pallas as pl
from jax.experimental.pallas import tpu as pltpu
from jax.sharding import PartitionSpec as P

HD = 128
B = 128
LEVELS = 6
MESH = pl.DeviceIdType.MESH
BF = jnp.bfloat16
F32 = jnp.float32
UNIT = math.log2(math.e) / math.sqrt(HD)


def reversed_bits(x, bits=7):
    out = jnp.zeros_like(x)
    for i in range(bits):
        out = out + (((x >> i) & 1) << (bits - 1 - i))
    return out


def dot(a, b):
    return jnp.dot(a, b, preferred_element_type=F32)


def pool_halves(x, blocks):
    rows, cols = x.shape
    y = x.reshape(blocks, 2, rows // (2 * blocks), cols)
    y = (y[:, 0] + y[:, 1]) * 0.5
    return y.reshape(rows // 2, cols).astype(BF)


def twice(x, blocks):
    rows, cols = x.shape
    y = x.reshape(blocks, rows // blocks, cols)
    return jnp.concatenate([y, y], axis=1).reshape(2 * rows, cols)


def attend(q, k, v, bias=None):
    s = lax.dot_general(q, k, (((1,), (1,)), ((), ())), preferred_element_type=F32)
    if bias is not None:
        s = s + bias
    top = jnp.max(s, axis=-1, keepdims=True)
    w = jnp.exp2((s - top) * UNIT).astype(BF)
    both = dot(w, jnp.concatenate([v, jnp.ones_like(v)], axis=1))
    return jnp.broadcast_to(top * UNIT, (q.shape[0], HD)), both[:, HD:], both[:, :HD]


def merge(a, b):
    top = jnp.maximum(a[0], b[0])
    ka, kb = jnp.exp2(a[0] - top), jnp.exp2(b[0] - top)
    return top, a[1] * ka + b[1] * kb, a[2] * ka + b[2] * kb


def group(level):
    return 1 << (level - 2)


def siblings(me, level):
    g = group(level)
    own = me // g
    base = (own + 1 - 2 * (own % 2)) * g
    return [base + (me + k) % g for k in range(g)]


def kernel(
    count,
    tok_hbm, wqk_hbm, wv_hbm, start_hbm, end_hbm,
    out_ref,
    tok_raw, tokp, wqk, wv, wq_s, wk_s, acc,
    q0, k0, v0, q1, k1, v1, q2, q3, q4,
    s2, s3, s4, s5, s6,
    r2, r3, r4, r5, r6, rq, sr, rr,
    fpeak, ftot, fnum,
    start_ref, end_ref, load_sem, send_sem, recv_sem,
):
    me, core = lax.axis_index("seq"), lax.axis_index("head")
    heads = q0.shape[0]
    sends = {2: s2, 3: s3, 4: s4, 5: s5, 6: s6}
    lands = {2: r2, 3: r3, 4: r4, 5: r5, 6: r6}

    loads = [
        pltpu.make_async_copy(tok_hbm, tok_raw, load_sem.at[0]),
        pltpu.make_async_copy(wqk_hbm, wqk, load_sem.at[1]),
        pltpu.make_async_copy(wv_hbm, wv, load_sem.at[2]),
        pltpu.make_async_copy(start_hbm, start_ref, load_sem.at[3]),
        pltpu.make_async_copy(end_hbm, end_ref, load_sem.at[4]),
    ]
    for load in loads:
        load.start()

    right, left = (me + 1) % count, (me + count - 1) % count
    twin = (me, 1 - core)
    greet = [twin, (right, core), (left, core)]
    for level in range(2, LEVELS + 1):
        greet += [(p, core) for p in siblings(me, level)]
    barrier = pltpu.get_barrier_semaphore()
    for device in greet:
        pl.semaphore_signal(barrier, inc=1, device_id=device, device_id_type=MESH)

    row = lax.broadcasted_iota(jnp.int32, (B, B), 0)
    col = lax.broadcasted_iota(jnp.int32, (B, B), 1)
    perm = jnp.where(reversed_bits(row) == col, 1.0, 0.0).astype(BF)

    loads[0].wait()
    for b in range(4):
        tokp[core, b + 1] = dot(perm, tok_raw[b * B : (b + 1) * B]).astype(BF)

    pl.semaphore_wait(barrier, len(greet))

    def send(src, dst, sem, device):
        copy = pltpu.make_async_remote_copy(
            src_ref=src, dst_ref=dst, send_sem=send_sem.at[sem], recv_sem=recv_sem.at[sem],
            device_id=device, device_id_type=MESH,
        )
        copy.start()
        return copy

    swap = send(tokp.at[core, pl.ds(1, 4)], tokp.at[core, pl.ds(1, 4)], 0, twin)
    to_right = send(tokp.at[core, 4], tokp.at[core, 0], 1, (right, core))
    to_left = send(tokp.at[core, 1], tokp.at[core, 5], 7, (left, core))

    loads[1].wait()

    def split(i, carry):
        rows = pl.ds(pl.multiple_of(i * 64, 64), 64)
        pair = jnp.swapaxes(wqk[rows], 0, 1)
        wq_s[rows, :] = pair[0]
        wk_s[rows, :] = pair[1]
        return carry

    lax.fori_loop(0, wqk.shape[0] // 64, split, 0)
    loads[2].wait()

    half = pl.multiple_of(core * 512, 512)
    other = pl.multiple_of((1 - core) * 512, 512)
    weights = (wk_s, wv, wq_s)
    mine = tokp[core, 1:5].reshape(4 * B, 512)
    for i, w in enumerate(weights):
        acc[i] = dot(mine, w[pl.ds(half, 512), :])

    swap.wait()
    theirs = tokp[1 - core, 1:5].reshape(4 * B, 512)

    def mix(apart):
        return jnp.where((col == row) | (col == (row ^ apart)), 0.5, 0.0).astype(BF)

    def narrow():
        r = lax.broadcasted_iota(jnp.int32, (16, 32), 0)
        c = lax.broadcasted_iota(jnp.int32, (16, 32), 1)
        first = (r // 4) * 8 + r % 4
        five = jnp.where((c == first) | (c == first + 4), 0.5, 0.0).astype(BF)
        r = lax.broadcasted_iota(jnp.int32, (8, 16), 0)
        c = lax.broadcasted_iota(jnp.int32, (8, 16), 1)
        first = (r // 2) * 4 + r % 2
        six = jnp.where((c == first) | (c == first + 2), 0.5, 0.0).astype(BF)
        return five, six

    five, six = narrow()
    last = {}
    for i in range(2):
        full = (acc[i] + dot(theirs, weights[i][pl.ds(other, 512), :])).astype(BF)
        x = full.astype(F32)
        store0, store1 = (k0, k1) if i == 0 else (v0, v1)
        for h in range(heads):
            cols = slice(h * HD, (h + 1) * HD)
            store0[h, B : 5 * B] = full[:, cols]
        l1 = pool_halves(x, 4)
        l2 = pool_halves(l1.astype(F32), 4)
        l3 = pool_halves(l2.astype(F32), 4)
        l4 = pool_halves(l3.astype(F32), 4)
        l5 = dot(five, l4).astype(BF)
        l6 = dot(six, l5)
        for h in range(heads):
            cols = slice(h * HD, (h + 1) * HD)
            store1[h] = l1[:, cols]
            s2[h, i] = l2[:, cols]
            s3[h, i] = l3[:, cols]
            s4[h, i] = l4[:, cols]
            s5[h, i] = l5[:, cols]
        last[i] = l6
    both = jnp.concatenate([last[0], last[1]], axis=0).astype(BF)
    for h in range(heads):
        s6[h] = both[:, h * HD : (h + 1) * HD]

    for level in range(LEVELS, 3, -1):
        for p in siblings(me, level):
            send(sends[level].at[p % 4], lands[level].at[me % group(level)], level, (p, core))
    for p in siblings(me, 3):
        send(s3, r3.at[me % 2], 3, (p, core))
    send(s2, r2, 2, (siblings(me, 2)[0], core))

    full = (acc[2] + dot(theirs, wq_s[pl.ds(other, 512), :])).astype(BF)
    l1 = pool_halves(full.astype(F32), 4)
    l2 = pool_halves(l1.astype(F32), 4)
    l3 = pool_halves(l2.astype(F32), 4)
    l4 = pool_halves(l3.astype(F32), 4)
    for h in range(heads):
        cols = slice(h * HD, (h + 1) * HD)
        q0[h] = full[:, cols]
        q1[h] = l1[:, cols]
        q2[h] = l2[:, cols]
        q3[h] = l3[:, cols]
        q4[h] = l4[:, cols]
    mine4 = me % 4
    mates = [me - mine4 + (mine4 + k) % 4 for k in range(1, 4)]
    for p in mates:
        send(q4.at[p % 4], rq.at[mine4], 10, (p, core))
    rq[mine4] = q4[mine4]

    to_right.wait_recv()
    relay_left = send(tokp.at[core, 0], tokp.at[core, 0], 8, twin)
    to_left.wait_recv()
    relay_right = send(tokp.at[core, 5], tokp.at[core, 5], 9, twin)
    relay_left.wait_recv()
    relay_right.wait_recv()

    for store, w in ((k0, wk_s), (v0, wv)):
        for b in (0, 5):
            full = dot(tokp[core, b], w[pl.ds(half, 512), :]) + dot(
                tokp[1 - core, b], w[pl.ds(other, 512), :]
            )
            full = full.astype(BF)
            for h in range(heads):
                store[h, b * B : (b + 1) * B] = full[:, h * HD : (h + 1) * HD]

    def landed(level):
        n = lands[level]
        pltpu.make_async_copy(n, n, recv_sem.at[level]).wait()

    landed(6)
    landed(5)
    landed(4)
    pltpu.make_async_copy(rq.at[pl.ds(0, 3)], rq.at[pl.ds(0, 3)], recv_sem.at[10]).wait()
    four = rq[...].reshape(B, HD)
    five = dot(mix(4), four).astype(BF)
    six = dot(mix(2), five).astype(BF)
    pairs = r6[...].astype(F32).reshape(16, 2, 8, HD)
    state = attend(six, pairs[:, 0].reshape(B, HD).astype(BF), pairs[:, 1].reshape(B, HD).astype(BF))
    state = merge(attend(five, r5[:, 0].reshape(B, HD), r5[:, 1].reshape(B, HD)), state)
    state = merge(attend(four, r4[:, 0].reshape(B, HD), r4[:, 1].reshape(B, HD)), state)
    line = [jnp.sum(jnp.where(row == col, x, 0.0), axis=0, keepdims=True) for x in state[:2]]
    stats = jnp.where(row[:8] == 0, line[0], line[1])
    for j in range(4):
        sr[j, :32] = state[2][j * 32 : (j + 1) * 32]
        sr[j, 32:] = stats
    for p in mates:
        send(sr.at[p % 4], rr.at[mine4], 11, (p, core))
    rr[mine4] = sr[mine4]

    place = reversed_bits(lax.broadcasted_iota(jnp.int32, (1, B), 1))
    none = jnp.zeros((1, B), F32)
    loads[3].wait()
    loads[4].wait()
    biases = []
    for b in range(4):
        before = (me * 4 + b - 1) * B + place
        after = (me * 4 + b + 1) * B + place
        biases.append(
            jnp.concatenate(
                [
                    jnp.where(before >= start_ref[b], 0.0, -jnp.inf),
                    none,
                    jnp.where(after < end_ref[b], 0.0, -jnp.inf),
                ],
                axis=1,
            )
        )

    def near(h, carry):
        for b in range(4):
            c = b // 2
            o = (c ^ 1) * B
            rows = slice(b * B, (b + 1) * B)
            fine = attend(q0[h, rows], k0[h, b * B : (b + 3) * B], v0[h, b * B : (b + 3) * B], biases[b])
            coarse = attend(q1[h, b * 64 : (b + 1) * 64], k1[h, o : o + B], v1[h, o : o + B])
            state = merge(fine, tuple(twice(x, 1) for x in coarse))
            fpeak[h, rows], ftot[h, rows], fnum[h, rows] = state
        return carry

    lax.fori_loop(0, heads, near, 0)

    landed(3)
    pltpu.make_async_copy(rr.at[pl.ds(0, 3)], rr.at[pl.ds(0, 3)], recv_sem.at[11]).wait()
    landed(2)

    def far(h, carry):
        own = col[:32] == mine4 * 32 + row[:32]
        stats = [
            jnp.sum(jnp.where(own, rr[h, 32 + i : 33 + i], 0.0), axis=1, keepdims=True)
            for i in range(2)
        ]
        state = tuple(jnp.broadcast_to(x, (32, HD)) for x in stats) + (rr[h, :32],)
        state = tuple(twice(x, 4) for x in state)
        state = merge(attend(q3[h], r3[:, h, 0].reshape(B, HD), r3[:, h, 1].reshape(B, HD)), state)
        state = tuple(twice(x, 4) for x in state)
        state = merge(attend(q2[h], r2[h, 0], r2[h, 1]), state)
        cols = pl.ds(pl.multiple_of(h * HD, HD), HD)
        for b in range(4):
            rows = slice(b * B, (b + 1) * B)
            part = tuple(twice(twice(x[b * 32 : (b + 1) * 32], 1), 1) for x in state)
            peak, total, numer = merge((fpeak[h, rows], ftot[h, rows], fnum[h, rows]), part)
            out_ref[rows, cols] = dot(perm, (numer / total).astype(BF)).astype(BF)
        return carry

    lax.fori_loop(0, heads, far, 0)

    to_right.wait_send()
    to_left.wait_send()
    relay_left.wait_send()
    relay_right.wait_send()
    for level in range(2, LEVELS + 1):
        n = lands[level]
        pltpu.make_async_copy(n, n, send_sem.at[level]).wait()
    pltpu.make_async_copy(rq.at[pl.ds(0, 3)], rq.at[pl.ds(0, 3)], send_sem.at[10]).wait()
    pltpu.make_async_copy(sr.at[pl.ds(0, 3)], sr.at[pl.ds(0, 3)], send_sem.at[11]).wait()


def on_device(count, tokens, w_qk, w_value, span_start, span_end):
    rows, feats = tokens.shape
    heads = w_value.shape[1] // HD
    anywhere = pl.BlockSpec(memory_space=pltpu.HBM)

    def vm(*shape, dtype=BF):
        return pltpu.VMEM(shape, dtype)

    width = heads * HD
    scratch = [
        vm(rows, feats), vm(2, 6, B, feats), vm(2 * feats, 2, width), vm(2 * feats, width),
        vm(2 * feats, width), vm(2 * feats, width), vm(3, rows, width, dtype=F32),
        vm(heads, rows, HD), vm(heads, rows + 2 * B, HD), vm(heads, rows + 2 * B, HD),
        vm(heads, 256, HD), vm(heads, 256, HD), vm(heads, 256, HD),
        vm(heads, 128, HD), vm(heads, 64, HD), vm(heads, 32, HD),
        vm(heads, 2, 128, HD), vm(heads, 2, 64, HD), vm(heads, 2, 32, HD), vm(heads, 2, 16, HD), vm(heads, 16, HD),
        vm(heads, 2, 128, HD), vm(2, heads, 2, 64, HD), vm(4, 2, 32, HD), vm(8, 2, 16, HD), vm(16, 16, HD),
        vm(4, 32, HD), vm(4, 40, HD, dtype=F32), vm(heads, 40, HD, dtype=F32),
        vm(heads, rows, HD, dtype=F32), vm(heads, rows, HD, dtype=F32), vm(heads, rows, HD, dtype=F32),
        pltpu.SMEM((4,), jnp.int32), pltpu.SMEM((4,), jnp.int32),
        pltpu.SemaphoreType.DMA((5,)), pltpu.SemaphoreType.DMA((12,)), pltpu.SemaphoreType.DMA((12,)),
    ]
    return pl.pallas_call(
        functools.partial(kernel, count),
        out_shape=jax.ShapeDtypeStruct((rows, width), BF),
        in_specs=[anywhere] * 5,
        out_specs=pl.BlockSpec(memory_space=pltpu.VMEM),
        scratch_shapes=scratch,
        name="htransformer",
        cost_estimate=pl.CostEstimate(flops=3 * 10**9, bytes_accessed=5 * 10**6, transcendentals=10**6),
        compiler_params=pltpu.CompilerParams(
            collective_id=0, has_side_effects=True, vmem_limit_bytes=56 * 2**20
        ),
    )(tokens, w_qk, w_value, span_start, span_end)


def solution(mesh):
    placed = (P("seq", "head"), P(None, None, "head"), P(None, "head"), P("seq"), P("seq"))
    return jax.shard_map(
        functools.partial(on_device, mesh.shape["seq"]),
        mesh=mesh, in_specs=placed, out_specs=P("seq", "head"), check_vma=False,
    )
```

```python
import functools
import math

import jax
import jax.numpy as jnp
from jax import lax
from jax.experimental import pallas as pl
from jax.experimental.pallas import tpu as pltpu
from jax.sharding import PartitionSpec as P

HD = 128
B = 128
NEAR_FIRST = 2
MESH = pl.DeviceIdType.MESH
BF = jnp.bfloat16
F32 = jnp.float32
UNIT = math.log2(math.e) / math.sqrt(HD)


def reversed_bits(x, bits=7):
    out = jnp.zeros_like(x)
    for i in range(bits):
        out = out + (((x >> i) & 1) << (bits - 1 - i))
    return out


def dot(a, b):
    return jnp.dot(a, b, preferred_element_type=F32)


def pool_halves(x, blocks):
    rows, cols = x.shape
    y = x.reshape(blocks, 2, rows // (2 * blocks), cols)
    y = (y[:, 0] + y[:, 1]) * 0.5
    return y.reshape(rows // 2, cols).astype(BF)


def twice(x, blocks):
    rows, cols = x.shape
    y = x.reshape(blocks, rows // blocks, cols)
    return jnp.concatenate([y, y], axis=1).reshape(2 * rows, cols)


def attend(q, k, v, bias=None):
    s = lax.dot_general(q, k, (((1,), (1,)), ((), ())), preferred_element_type=F32)
    if bias is not None:
        s = s + bias
    top = jnp.max(s, axis=-1, keepdims=True)
    w = jnp.exp2((s - top) * UNIT).astype(BF)
    both = dot(w, jnp.concatenate([v, jnp.ones_like(v)], axis=1))
    return jnp.broadcast_to(top * UNIT, (q.shape[0], HD)), both[:, HD:], both[:, :HD]


def merge(a, b):
    top = jnp.maximum(a[0], b[0])
    ka, kb = jnp.exp2(a[0] - top), jnp.exp2(b[0] - top)
    return top, a[1] * ka + b[1] * kb, a[2] * ka + b[2] * kb


def pool_matrix(rows, run):
    r = lax.broadcasted_iota(jnp.int32, (rows, 2 * rows), 0)
    c = lax.broadcasted_iota(jnp.int32, (rows, 2 * rows), 1)
    first = (r // run) * (2 * run) + r % run
    return jnp.where((c == first) | (c == first + run), 0.5, 0.0).astype(BF)


def kernel(
    count,
    tok_hbm, wqk_hbm, wv_hbm, span_hbm,
    out_ref,
    tok_raw, tokp, wqk, wv, wq_s, wk_s, acc,
    q0, k0, v0, q1, k1, v1, q2,
    s2, s3, s4, s5, s6, sr,
    r2, r3, r4, r5, r6, rr,
    fpeak, ftot, fnum,
    span, load_sem, send_sem, recv_sem,
):
    me, core = lax.axis_index("seq"), lax.axis_index("head")
    heads = q0.shape[0]

    loads = [
        pltpu.make_async_copy(tok_hbm, tok_raw, load_sem.at[0]),
        pltpu.make_async_copy(wqk_hbm, wqk, load_sem.at[1]),
        pltpu.make_async_copy(wv_hbm, wv, load_sem.at[2]),
        pltpu.make_async_copy(span_hbm, span, load_sem.at[3]),
    ]
    for load in loads:
        load.start()

    def flip(device, bit):
        return device + bit * (1 - 2 * ((device // bit) % 2))

    def mirror(device):
        return device + 7 - 2 * (device % 8)

    def head_of(device):
        place = device % 4
        return place + ((device // 4) % 2) * (3 - 2 * place)

    right, left = (me + 1) % count, (me + count - 1) % count
    twin = (me, 1 - core)
    place4 = me % 4
    mates = [me - place4 + (place4 + k) % 4 for k in (1, 2, 3)]
    over5 = [flip(me, 8), mirror(flip(me, 8))]
    across = flip(me, 16)
    over6 = [across, flip(across, 8), mirror(across), mirror(flip(across, 8))]
    greet = [twin] + [(p, core) for p in [right, left, mirror(me)] + mates + over5 + over6]
    barrier = pltpu.get_barrier_semaphore()
    for device in greet:
        pl.semaphore_signal(barrier, inc=1, device_id=device, device_id_type=MESH)

    row = lax.broadcasted_iota(jnp.int32, (B, B), 0)
    col = lax.broadcasted_iota(jnp.int32, (B, B), 1)
    perm = jnp.where(reversed_bits(row) == col, 1.0, 0.0).astype(BF)

    loads[0].wait()
    for b in range(4):
        tokp[core, b + 1] = dot(perm, tok_raw[b * B : (b + 1) * B]).astype(BF)

    pl.semaphore_wait(barrier, len(greet))

    def send(src, dst, sem, device):
        copy = pltpu.make_async_remote_copy(
            src_ref=src, dst_ref=dst, send_sem=send_sem.at[sem], recv_sem=recv_sem.at[sem],
            device_id=device, device_id_type=MESH,
        )
        copy.start()
        return copy

    def arrived(ref, sem):
        pltpu.make_async_copy(ref, ref, recv_sem.at[sem]).wait()

    def gone(ref, sem):
        pltpu.make_async_copy(ref, ref, send_sem.at[sem]).wait()

    swap = send(tokp.at[core, pl.ds(1, 4)], tokp.at[core, pl.ds(1, 4)], 0, twin)
    to_right = send(tokp.at[core, 4], tokp.at[core, 0], 1, (right, core))
    to_left = send(tokp.at[core, 1], tokp.at[core, 5], 7, (left, core))

    loads[1].wait()

    def split(i, carry):
        rows = pl.ds(pl.multiple_of(i * 64, 64), 64)
        pair = jnp.swapaxes(wqk[rows], 0, 1)
        wq_s[rows, :] = pair[0]
        wk_s[rows, :] = pair[1]
        return carry

    lax.fori_loop(0, wqk.shape[0] // 64, split, 0)
    loads[2].wait()

    half = pl.multiple_of(core * 512, 512)
    other = pl.multiple_of((1 - core) * 512, 512)
    weights = (wk_s, wv, wq_s)
    mine = tokp[core, 1:5].reshape(4 * B, 512)
    for i, w in enumerate(weights):
        acc[i] = dot(mine, w[pl.ds(half, 512), :])

    swap.wait()
    theirs = tokp[1 - core, 1:5].reshape(4 * B, 512)

    for i in range(3):
        full = (acc[i] + dot(theirs, weights[i][pl.ds(other, 512), :])).astype(BF)
        l1 = pool_halves(full.astype(F32), 4)
        l2 = pool_halves(l1.astype(F32), 4)
        l3 = pool_halves(l2.astype(F32), 4)
        for h in range(heads):
            cols = slice(h * HD, (h + 1) * HD)
            s3[h, i] = l3[:, cols]
            if i < 2:
                (k0, v0)[i][h, B : 5 * B] = full[:, cols]
                (k1, v1)[i][h] = l1[:, cols]
                s2[h, i] = l2[:, cols]
            else:
                q0[h] = full[:, cols]
                q1[h] = l1[:, cols]
                q2[h] = l2[:, cols]

    my_head = head_of(me)
    for p in mates:
        send(s3.at[head_of(p)], r3.at[place4], 3, (p, core))
    send(s2, r2, 2, (flip(me, 1), core))
    r3[place4] = s3[my_head]

    to_right.wait_recv()
    relay_left = send(tokp.at[core, 0], tokp.at[core, 0], 8, twin)
    to_left.wait_recv()
    relay_right = send(tokp.at[core, 5], tokp.at[core, 5], 9, twin)
    relay_left.wait_recv()
    relay_right.wait_recv()

    for store, w in ((k0, wk_s), (v0, wv)):
        for b in (0, 5):
            full = dot(tokp[core, b], w[pl.ds(half, 512), :]) + dot(
                tokp[1 - core, b], w[pl.ds(other, 512), :]
            )
            full = full.astype(BF)
            for h in range(heads):
                store[h, b * B : (b + 1) * B] = full[:, h * HD : (h + 1) * HD]

    turned = reversed_bits(lax.broadcasted_iota(jnp.int32, (1, B), 1))
    none = jnp.zeros((1, B), F32)
    loads[3].wait()
    biases = []
    for b in range(4):
        before = (me * 4 + b - 1) * B + turned
        after = (me * 4 + b + 1) * B + turned
        biases.append(
            jnp.concatenate(
                [
                    jnp.where(before >= span[0, b], 0.0, -jnp.inf),
                    none,
                    jnp.where(after < span[1, b], 0.0, -jnp.inf),
                ],
                axis=1,
            )
        )

    def near(h, carry):
        for b in range(4):
            c = b // 2
            o = (c ^ 1) * B
            rows = slice(b * B, (b + 1) * B)
            fine = attend(q0[h, rows], k0[h, b * B : (b + 3) * B], v0[h, b * B : (b + 3) * B], biases[b])
            coarse = attend(q1[h, b * 64 : (b + 1) * 64], k1[h, o : o + B], v1[h, o : o + B])
            state = merge(fine, tuple(twice(x, 1) for x in coarse))
            fpeak[h, rows], ftot[h, rows], fnum[h, rows] = state
        return carry

    lax.fori_loop(0, NEAR_FIRST, near, 0)

    arrived(r3.at[pl.ds(0, 3)], 3)
    five_rows, six_rows = pool_matrix(64, 4), pool_matrix(32, 2)
    for i in range(2):
        l4 = pool_halves(r3[:, i].astype(F32).reshape(2 * B, HD), 16)
        l5 = dot(five_rows, l4).astype(BF)
        s4[i] = l4
        s5[i] = l5
        s6[i] = dot(six_rows, l5).astype(BF)
    for p in over6:
        send(s6, r6.at[(me // 4) % 4], 6, (p, core))
    for p in over5:
        send(s5, r5.at[(me // 4) % 2], 5, (p, core))
    send(s4, r4, 4, (mirror(me), core))

    queries = r3[:, 2]
    three = [
        attend(
            queries[2 * c : 2 * c + 2].reshape(B, HD),
            r3[2 - 2 * c : 4 - 2 * c, 0].reshape(B, HD),
            r3[2 - 2 * c : 4 - 2 * c, 1].reshape(B, HD),
        )
        for c in range(2)
    ]
    four = pool_halves(queries.astype(F32).reshape(2 * B, HD), 16)

    def mix(apart):
        return jnp.where((col == row) | (col == (row ^ apart)), 0.5, 0.0).astype(BF)

    five = dot(mix(4), four).astype(BF)
    six = dot(mix(2), five).astype(BF)

    lax.fori_loop(NEAR_FIRST, heads, near, 0)

    arrived(r2, 2)

    def second(h, carry):
        state = attend(q2[h], r2[h, 0], r2[h, 1])
        for b in range(4):
            rows = slice(b * B, (b + 1) * B)
            part = tuple(twice(twice(x[b * 32 : (b + 1) * 32], 1), 1) for x in state)
            peak, total, numer = merge((fpeak[h, rows], ftot[h, rows], fnum[h, rows]), part)
            fnum[h, rows] = numer / total
            fpeak[h, rows] = peak + jnp.log2(total)
        return carry

    lax.fori_loop(0, heads, second, 0)

    arrived(r6, 6)
    state = attend(six, r6[:, 0].reshape(B, HD), r6[:, 1].reshape(B, HD))
    arrived(r5, 5)
    state = merge(attend(five, r5[:, 0].reshape(B, HD), r5[:, 1].reshape(B, HD)), state)
    arrived(r4, 4)
    state = merge(attend(four, r4[0], r4[1]), state)
    lines = []
    for c in range(2):
        part = tuple(twice(x[c * 64 : (c + 1) * 64], 8) for x in state)
        peak, total, numer = merge(three[c], part)
        result = numer / total
        level = peak + jnp.log2(total)
        lines.append(jnp.sum(jnp.where(row == col, level, 0.0), axis=0, keepdims=True))
        sr[2 * c, :64] = result[:64]
        sr[2 * c + 1, :64] = result[64:]
    stats = jnp.where(row[:8] == 0, lines[0], lines[1])
    for j in range(4):
        sr[j, 64:] = stats
    for p in mates:
        send(sr.at[p % 4], rr.at[my_head], 10, (p, core))
    rr[my_head] = sr[place4]
    arrived(rr.at[pl.ds(0, 3)], 10)

    own = col[:64] == (place4 % 2) * 64 + row[:64]

    def last(h, carry):
        line = rr[h, pl.ds(64 + place4 // 2, 1)]
        level = jnp.sum(jnp.where(own, line, 0.0), axis=1, keepdims=True)
        level = jnp.broadcast_to(level, (64, HD))
        cols = pl.ds(pl.multiple_of(h * HD, HD), HD)
        for b in range(4):
            rows = slice(b * B, (b + 1) * B)
            far, far_level = rr[h, b * 16 : (b + 1) * 16], level[b * 16 : (b + 1) * 16]
            for _ in range(3):
                far, far_level = twice(far, 1), twice(far_level, 1)
            close = fnum[h, rows]
            share = 1.0 / (1.0 + jnp.exp2(fpeak[h, rows] - far_level))
            mixed = close + (far - close) * share
            out_ref[rows, cols] = dot(perm, mixed.astype(BF)).astype(BF)
        return carry

    lax.fori_loop(0, heads, last, 0)

    to_right.wait_send()
    to_left.wait_send()
    relay_left.wait_send()
    relay_right.wait_send()
    gone(r2, 2)
    gone(r3.at[pl.ds(0, 3)], 3)
    gone(r4, 4)
    gone(r5, 5)
    gone(r6, 6)
    gone(rr.at[pl.ds(0, 3)], 10)


def on_device(count, tokens, w_qk, w_value, span_start, span_end):
    rows, feats = tokens.shape
    heads = w_value.shape[1] // HD
    anywhere = pl.BlockSpec(memory_space=pltpu.HBM)

    def vm(*shape, dtype=BF):
        return pltpu.VMEM(shape, dtype)

    width = heads * HD
    scratch = [
        vm(rows, feats), vm(2, 6, B, feats), vm(2 * feats, 2, width), vm(2 * feats, width),
        vm(2 * feats, width), vm(2 * feats, width), vm(3, rows, width, dtype=F32),
        vm(heads, rows, HD), vm(heads, rows + 2 * B, HD), vm(heads, rows + 2 * B, HD),
        vm(heads, 256, HD), vm(heads, 256, HD), vm(heads, 256, HD), vm(heads, 128, HD),
        vm(heads, 2, 128, HD), vm(heads, 3, 64, HD), vm(2, 128, HD), vm(2, 64, HD), vm(2, 32, HD),
        vm(4, 72, HD, dtype=F32),
        vm(heads, 2, 128, HD), vm(4, 3, 64, HD), vm(2, 128, HD), vm(2, 2, 64, HD), vm(4, 2, 32, HD),
        vm(heads, 72, HD, dtype=F32),
        vm(heads, rows, HD, dtype=F32), vm(heads, rows, HD, dtype=F32), vm(heads, rows, HD, dtype=F32),
        pltpu.SMEM((2, 4), jnp.int32),
        pltpu.SemaphoreType.DMA((4,)), pltpu.SemaphoreType.DMA((11,)), pltpu.SemaphoreType.DMA((11,)),
    ]
    return pl.pallas_call(
        functools.partial(kernel, count),
        out_shape=jax.ShapeDtypeStruct((rows, width), BF),
        in_specs=[anywhere] * 4,
        out_specs=pl.BlockSpec(memory_space=pltpu.VMEM),
        scratch_shapes=scratch,
        name="htransformer",
        cost_estimate=pl.CostEstimate(flops=3 * 10**9, bytes_accessed=5 * 10**6, transcendentals=10**6),
        compiler_params=pltpu.CompilerParams(
            collective_id=0, has_side_effects=True, vmem_limit_bytes=53 * 2**20
        ),
    )(tokens, w_qk, w_value, jnp.stack([span_start, span_end]))


def solution(mesh):
    placed = (P("seq", "head"), P(None, None, "head"), P(None, "head"), P("seq"), P("seq"))
    return jax.shard_map(
        functools.partial(on_device, mesh.shape["seq"]),
        mesh=mesh, in_specs=placed, out_specs=P("seq", "head"), check_vma=False,
    )
```

```python
import functools
import math

import jax
import jax.numpy as jnp
from jax import lax
from jax.experimental import pallas as pl
from jax.experimental.pallas import tpu as pltpu
from jax.sharding import PartitionSpec as P

HD = 128
B = 128
NEAR_FIRST = 2
MESH = pl.DeviceIdType.MESH
BF = jnp.bfloat16
F32 = jnp.float32
UNIT = math.log2(math.e) / math.sqrt(HD)


def reversed_bits(x, bits=7):
    out = jnp.zeros_like(x)
    for i in range(bits):
        out = out + (((x >> i) & 1) << (bits - 1 - i))
    return out


def dot(a, b):
    return jnp.dot(a, b, preferred_element_type=F32)


def pool_halves(x, blocks):
    rows, cols = x.shape
    y = x.reshape(blocks, 2, rows // (2 * blocks), cols)
    y = (y[:, 0] + y[:, 1]) * 0.5
    return y.reshape(rows // 2, cols).astype(BF)


def twice(x, blocks):
    rows, cols = x.shape
    y = x.reshape(blocks, rows // blocks, cols)
    return jnp.concatenate([y, y], axis=1).reshape(2 * rows, cols)


def attend(q, k, v, bias=None):
    s = lax.dot_general(q, k, (((1,), (1,)), ((), ())), preferred_element_type=F32)
    if bias is not None:
        s = s + bias
    top = jnp.max(s, axis=-1, keepdims=True)
    w = jnp.exp2((s - top) * UNIT).astype(BF)
    both = dot(w, jnp.concatenate([v, jnp.ones_like(v)], axis=1))
    return jnp.broadcast_to(top * UNIT, (q.shape[0], HD)), both[:, HD:], both[:, :HD]


def merge(a, b):
    top = jnp.maximum(a[0], b[0])
    ka, kb = jnp.exp2(a[0] - top), jnp.exp2(b[0] - top)
    return top, a[1] * ka + b[1] * kb, a[2] * ka + b[2] * kb


def pool_matrix(rows, run):
    r = lax.broadcasted_iota(jnp.int32, (rows, 2 * rows), 0)
    c = lax.broadcasted_iota(jnp.int32, (rows, 2 * rows), 1)
    first = (r // run) * (2 * run) + r % run
    return jnp.where((c == first) | (c == first + run), 0.5, 0.0).astype(BF)


def kernel(
    count,
    tok_hbm, wqk_hbm, wv_hbm, span_hbm,
    out_ref,
    raw, tokp, wqk, wv, wq_s, wk_s, acc,
    q0, k0, v0, q1, k1, v1, q2,
    s2, s3, s4, s5, s6, sr,
    r2, r3, r4, r5, r6, rr,
    fpeak, ftot, fnum,
    span, load_sem, send_sem, recv_sem,
):
    me, core = lax.axis_index("seq"), lax.axis_index("head")
    heads, rows = q0.shape[0], q0.shape[1]

    loads = [
        pltpu.make_async_copy(tok_hbm, raw.at[core, pl.ds(B, rows)], load_sem.at[0]),
        pltpu.make_async_copy(wqk_hbm, wqk, load_sem.at[1]),
        pltpu.make_async_copy(wv_hbm, wv, load_sem.at[2]),
        pltpu.make_async_copy(span_hbm, span, load_sem.at[3]),
    ]
    for load in loads:
        load.start()

    def flip(device, bit):
        return device + bit * (1 - 2 * ((device // bit) % 2))

    def mirror(device):
        return device + 7 - 2 * (device % 8)

    def head_of(device):
        place = device % 4
        return place + ((device // 4) % 2) * (3 - 2 * place)

    right, left = (me + 1) % count, (me + count - 1) % count
    twin = (me, 1 - core)
    place4 = me % 4
    mates = [me - place4 + (place4 + k) % 4 for k in (1, 2, 3)]
    over5 = [flip(me, 8), mirror(flip(me, 8))]
    across = flip(me, 16)
    over6 = [across, flip(across, 8), mirror(across), mirror(flip(across, 8))]
    greet = [twin] + [(p, core) for p in [right, left, mirror(me)] + mates + over5 + over6]
    barrier = pltpu.get_barrier_semaphore()
    for device in greet:
        pl.semaphore_signal(barrier, inc=1, device_id=device, device_id_type=MESH)

    row = lax.broadcasted_iota(jnp.int32, (B, B), 0)
    col = lax.broadcasted_iota(jnp.int32, (B, B), 1)
    perm = jnp.where(reversed_bits(row) == col, 1.0, 0.0).astype(BF)

    pl.semaphore_wait(barrier, len(greet))

    def send(src, dst, sem, device):
        copy = pltpu.make_async_remote_copy(
            src_ref=src, dst_ref=dst, send_sem=send_sem.at[sem], recv_sem=recv_sem.at[sem],
            device_id=device, device_id_type=MESH,
        )
        copy.start()
        return copy

    def arrived(ref, sem):
        pltpu.make_async_copy(ref, ref, recv_sem.at[sem]).wait()

    def gone(ref, sem):
        pltpu.make_async_copy(ref, ref, send_sem.at[sem]).wait()

    swap = send(tok_hbm, raw.at[core, pl.ds(B, rows)], 0, twin)
    to_right = send(tok_hbm.at[pl.ds(rows - B, B)], raw.at[core, pl.ds(0, B)], 1, (right, core))
    to_left = send(tok_hbm.at[pl.ds(0, B)], raw.at[core, pl.ds(rows + B, B)], 7, (left, core))

    def turn(side, b):
        tokp[side, b] = dot(perm, raw[side, b * B : (b + 1) * B]).astype(BF)

    loads[0].wait()
    for b in range(1, 5):
        turn(core, b)
    loads[1].wait()

    def split(i, carry):
        rows = pl.ds(pl.multiple_of(i * 64, 64), 64)
        pair = jnp.swapaxes(wqk[rows], 0, 1)
        wq_s[rows, :] = pair[0]
        wk_s[rows, :] = pair[1]
        return carry

    lax.fori_loop(0, wqk.shape[0] // 64, split, 0)
    loads[2].wait()

    half = pl.multiple_of(core * 512, 512)
    other = pl.multiple_of((1 - core) * 512, 512)
    weights = (wk_s, wv, wq_s)
    mine = tokp[core, 1:5].reshape(4 * B, 512)
    for i, w in enumerate(weights):
        acc[i] = dot(mine, w[pl.ds(half, 512), :])

    swap.wait()
    for b in range(1, 5):
        turn(1 - core, b)
    theirs = tokp[1 - core, 1:5].reshape(4 * B, 512)

    for i in range(3):
        full = (acc[i] + dot(theirs, weights[i][pl.ds(other, 512), :])).astype(BF)
        l1 = pool_halves(full.astype(F32), 4)
        l2 = pool_halves(l1.astype(F32), 4)
        l3 = pool_halves(l2.astype(F32), 4)
        for h in range(heads):
            cols = slice(h * HD, (h + 1) * HD)
            s3[h, i] = l3[:, cols]
            if i < 2:
                (k0, v0)[i][h, B : 5 * B] = full[:, cols]
                (k1, v1)[i][h] = l1[:, cols]
                s2[h, i] = l2[:, cols]
            else:
                q0[h] = full[:, cols]
                q1[h] = l1[:, cols]
                q2[h] = l2[:, cols]

    my_head = head_of(me)
    for p in mates:
        send(s3.at[head_of(p)], r3.at[place4], 3, (p, core))
    send(s2, r2, 2, (flip(me, 1), core))
    r3[place4] = s3[my_head]

    to_right.wait_recv()
    relay_left = send(raw.at[core, pl.ds(0, B)], raw.at[core, pl.ds(0, B)], 8, twin)
    to_left.wait_recv()
    relay_right = send(raw.at[core, pl.ds(rows + B, B)], raw.at[core, pl.ds(rows + B, B)], 9, twin)
    arrived(r3.at[pl.ds(0, 3)], 3)
    five_rows, six_rows = pool_matrix(64, 4), pool_matrix(32, 2)
    for i in range(2):
        l4 = pool_halves(r3[:, i].astype(F32).reshape(2 * B, HD), 16)
        l5 = dot(five_rows, l4).astype(BF)
        s4[i] = l4
        s5[i] = l5
        s6[i] = dot(six_rows, l5).astype(BF)
    for p in over6:
        send(s6, r6.at[(me // 4) % 4], 6, (p, core))
    for p in over5:
        send(s5, r5.at[(me // 4) % 2], 5, (p, core))
    send(s4, r4, 4, (mirror(me), core))

    queries = r3[:, 2]
    three = [
        attend(
            queries[2 * c : 2 * c + 2].reshape(B, HD),
            r3[2 - 2 * c : 4 - 2 * c, 0].reshape(B, HD),
            r3[2 - 2 * c : 4 - 2 * c, 1].reshape(B, HD),
        )
        for c in range(2)
    ]
    four = pool_halves(queries.astype(F32).reshape(2 * B, HD), 16)

    def mix(apart):
        return jnp.where((col == row) | (col == (row ^ apart)), 0.5, 0.0).astype(BF)

    five = dot(mix(4), four).astype(BF)
    six = dot(mix(2), five).astype(BF)

    relay_left.wait_recv()
    relay_right.wait_recv()
    for b in (0, 5):
        turn(core, b)
        turn(1 - core, b)

    for store, w in ((k0, wk_s), (v0, wv)):
        for b in (0, 5):
            full = dot(tokp[core, b], w[pl.ds(half, 512), :]) + dot(
                tokp[1 - core, b], w[pl.ds(other, 512), :]
            )
            full = full.astype(BF)
            for h in range(heads):
                store[h, b * B : (b + 1) * B] = full[:, h * HD : (h + 1) * HD]

    turned = reversed_bits(lax.broadcasted_iota(jnp.int32, (1, B), 1))
    none = jnp.zeros((1, B), F32)
    loads[3].wait()
    biases = []
    for b in range(4):
        before = (me * 4 + b - 1) * B + turned
        after = (me * 4 + b + 1) * B + turned
        biases.append(
            jnp.concatenate(
                [
                    jnp.where(before >= span[0, b], 0.0, -jnp.inf),
                    none,
                    jnp.where(after < span[1, b], 0.0, -jnp.inf),
                ],
                axis=1,
            )
        )

    def near(h, carry):
        for b in range(4):
            c = b // 2
            o = (c ^ 1) * B
            rows = slice(b * B, (b + 1) * B)
            fine = attend(q0[h, rows], k0[h, b * B : (b + 3) * B], v0[h, b * B : (b + 3) * B], biases[b])
            coarse = attend(q1[h, b * 64 : (b + 1) * 64], k1[h, o : o + B], v1[h, o : o + B])
            state = merge(fine, tuple(twice(x, 1) for x in coarse))
            fpeak[h, rows], ftot[h, rows], fnum[h, rows] = state
        return carry

    lax.fori_loop(0, NEAR_FIRST, near, 0)

    arrived(r6, 6)
    state = attend(six, r6[:, 0].reshape(B, HD), r6[:, 1].reshape(B, HD))
    arrived(r5, 5)
    state = merge(attend(five, r5[:, 0].reshape(B, HD), r5[:, 1].reshape(B, HD)), state)
    arrived(r4, 4)
    state = merge(attend(four, r4[0], r4[1]), state)
    lines = []
    for c in range(2):
        part = tuple(twice(x[c * 64 : (c + 1) * 64], 8) for x in state)
        peak, total, numer = merge(three[c], part)
        result = numer / total
        level = peak + jnp.log2(total)
        lines.append(jnp.sum(jnp.where(row == col, level, 0.0), axis=0, keepdims=True))
        sr[2 * c, :64] = result[:64]
        sr[2 * c + 1, :64] = result[64:]
    stats = jnp.where(row[:8] == 0, lines[0], lines[1])
    for j in range(4):
        sr[j, 64:] = stats
    for p in mates:
        send(sr.at[p % 4], rr.at[my_head], 10, (p, core))
    rr[my_head] = sr[place4]
    lax.fori_loop(NEAR_FIRST, heads, near, 0)
    arrived(r2, 2)

    def second(h, carry):
        state = attend(q2[h], r2[h, 0], r2[h, 1])
        for b in range(4):
            rows = slice(b * B, (b + 1) * B)
            part = tuple(twice(twice(x[b * 32 : (b + 1) * 32], 1), 1) for x in state)
            peak, total, numer = merge((fpeak[h, rows], ftot[h, rows], fnum[h, rows]), part)
            fnum[h, rows] = numer / total
            fpeak[h, rows] = peak + jnp.log2(total)
        return carry

    lax.fori_loop(0, heads, second, 0, unroll=True)

    arrived(rr.at[pl.ds(0, 3)], 10)

    own = col[:64] == (place4 % 2) * 64 + row[:64]

    def last(h, carry):
        line = rr[h, pl.ds(64 + place4 // 2, 1)]
        level = jnp.sum(jnp.where(own, line, 0.0), axis=1, keepdims=True)
        level = jnp.broadcast_to(level, (64, HD))
        cols = pl.ds(pl.multiple_of(h * HD, HD), HD)
        for b in range(4):
            rows = slice(b * B, (b + 1) * B)
            far, far_level = rr[h, b * 16 : (b + 1) * 16], level[b * 16 : (b + 1) * 16]
            for _ in range(3):
                far, far_level = twice(far, 1), twice(far_level, 1)
            close = fnum[h, rows]
            share = 1.0 / (1.0 + jnp.exp2(fpeak[h, rows] - far_level))
            mixed = close + (far - close) * share
            out_ref[rows, cols] = dot(perm, mixed.astype(BF)).astype(BF)
        return carry

    lax.fori_loop(0, heads, last, 0, unroll=True)

    to_right.wait_send()
    to_left.wait_send()
    relay_left.wait_send()
    relay_right.wait_send()
    gone(r2, 2)
    gone(r3.at[pl.ds(0, 3)], 3)
    gone(r4, 4)
    gone(r5, 5)
    gone(r6, 6)
    gone(rr.at[pl.ds(0, 3)], 10)


def on_device(count, tokens, w_qk, w_value, span_start, span_end):
    rows, feats = tokens.shape
    heads = w_value.shape[1] // HD
    anywhere = pl.BlockSpec(memory_space=pltpu.HBM)

    def vm(*shape, dtype=BF):
        return pltpu.VMEM(shape, dtype)

    width = heads * HD
    scratch = [
        vm(2, rows + 2 * B, feats), vm(2, 6, B, feats), vm(2 * feats, 2, width), vm(2 * feats, width),
        vm(2 * feats, width), vm(2 * feats, width), vm(3, rows, width, dtype=F32),
        vm(heads, rows, HD), vm(heads, rows + 2 * B, HD), vm(heads, rows + 2 * B, HD),
        vm(heads, 256, HD), vm(heads, 256, HD), vm(heads, 256, HD), vm(heads, 128, HD),
        vm(heads, 2, 128, HD), vm(heads, 3, 64, HD), vm(2, 128, HD), vm(2, 64, HD), vm(2, 32, HD),
        vm(4, 72, HD, dtype=F32),
        vm(heads, 2, 128, HD), vm(4, 3, 64, HD), vm(2, 128, HD), vm(2, 2, 64, HD), vm(4, 2, 32, HD),
        vm(heads, 72, HD, dtype=F32),
        vm(heads, rows, HD, dtype=F32), vm(heads, rows, HD, dtype=F32), vm(heads, rows, HD, dtype=F32),
        pltpu.SMEM((2, 4), jnp.int32),
        pltpu.SemaphoreType.DMA((4,)), pltpu.SemaphoreType.DMA((11,)), pltpu.SemaphoreType.DMA((11,)),
    ]
    return pl.pallas_call(
        functools.partial(kernel, count),
        out_shape=jax.ShapeDtypeStruct((rows, width), BF),
        in_specs=[anywhere] * 4,
        out_specs=pl.BlockSpec(memory_space=pltpu.VMEM),
        scratch_shapes=scratch,
        name="htransformer",
        cost_estimate=pl.CostEstimate(flops=3 * 10**9, bytes_accessed=5 * 10**6, transcendentals=10**6),
        compiler_params=pltpu.CompilerParams(
            collective_id=0, has_side_effects=True, vmem_limit_bytes=53 * 2**20
        ),
    )(tokens, w_qk, w_value, jnp.stack([span_start, span_end]))


def solution(mesh):
    placed = (P("seq", "head"), P(None, None, "head"), P(None, "head"), P("seq"), P("seq"))
    return jax.shard_map(
        functools.partial(on_device, mesh.shape["seq"]),
        mesh=mesh, in_specs=placed, out_specs=P("seq", "head"), check_vma=False,
    )
```

```python
import functools
import math

import jax
import jax.numpy as jnp
from jax import lax
from jax.experimental import pallas as pl
from jax.experimental.pallas import tpu as pltpu
from jax.sharding import PartitionSpec as P

HD = 128
B = 128
NEAR_FIRST = 2
MESH = pl.DeviceIdType.MESH
BF = jnp.bfloat16
F32 = jnp.float32
UNIT = math.log2(math.e) / math.sqrt(HD)


def reversed_bits(x, bits=7):
    out = jnp.zeros_like(x)
    for i in range(bits):
        out = out + (((x >> i) & 1) << (bits - 1 - i))
    return out


def dot(a, b):
    return jnp.dot(a, b, preferred_element_type=F32)


def pool_halves(x, blocks):
    rows, cols = x.shape
    y = x.reshape(blocks, 2, rows // (2 * blocks), cols)
    y = (y[:, 0] + y[:, 1]) * 0.5
    return y.reshape(rows // 2, cols).astype(BF)


def twice(x, blocks):
    rows, cols = x.shape
    y = x.reshape(blocks, rows // blocks, cols)
    return jnp.concatenate([y, y], axis=1).reshape(2 * rows, cols)


def attend(q, k, v, bias=None):
    s = lax.dot_general(q, k, (((1,), (1,)), ((), ())), preferred_element_type=F32)
    if bias is not None:
        s = s + bias
    top = jnp.max(s, axis=-1, keepdims=True)
    w = jnp.exp2((s - top) * UNIT).astype(BF)
    both = dot(w, jnp.concatenate([v, jnp.ones_like(v)], axis=1))
    return jnp.broadcast_to(top * UNIT, (q.shape[0], HD)), both[:, HD:], both[:, :HD]


def merge(a, b):
    top = jnp.maximum(a[0], b[0])
    ka, kb = jnp.exp2(a[0] - top), jnp.exp2(b[0] - top)
    return top, a[1] * ka + b[1] * kb, a[2] * ka + b[2] * kb


def pool_matrix(rows, run):
    r = lax.broadcasted_iota(jnp.int32, (rows, 2 * rows), 0)
    c = lax.broadcasted_iota(jnp.int32, (rows, 2 * rows), 1)
    first = (r // run) * (2 * run) + r % run
    return jnp.where((c == first) | (c == first + run), 0.5, 0.0).astype(BF)


def kernel(
    count,
    tok_hbm, wqk_hbm, wv_hbm, span_hbm,
    out_ref,
    raw, tokp, wqk, wv, wq_s, wk_s, acc,
    q0, k0, v0, q1, k1, v1, q2,
    s2, s3, sq, s4, s5, s6, sr,
    r2, r3, rq, r4, r5, r6, rr,
    fpeak, ftot, fnum,
    span, load_sem, send_sem, recv_sem,
):
    me, core = lax.axis_index("seq"), lax.axis_index("head")
    heads, rows = q0.shape[0], q0.shape[1]

    loads = [
        pltpu.make_async_copy(tok_hbm, raw.at[core, pl.ds(B, rows)], load_sem.at[0]),
        pltpu.make_async_copy(wqk_hbm, wqk, load_sem.at[1]),
        pltpu.make_async_copy(wv_hbm, wv, load_sem.at[2]),
        pltpu.make_async_copy(span_hbm, span, load_sem.at[3]),
    ]
    for load in loads:
        load.start()

    def flip(device, bit):
        return device + bit * (1 - 2 * ((device // bit) % 2))

    def mirror(device):
        return device + 7 - 2 * (device % 8)

    def head_of(device):
        place = device % 4
        return place + ((device // 4) % 2) * (3 - 2 * place)

    right, left = (me + 1) % count, (me + count - 1) % count
    twin = (me, 1 - core)
    place4 = me % 4
    mates = [me - place4 + (place4 + k) % 4 for k in (1, 2, 3)]
    over5 = [flip(me, 8), mirror(flip(me, 8))]
    across = flip(me, 16)
    over6 = [across, flip(across, 8), mirror(across), mirror(flip(across, 8))]
    greet = [twin] + [(p, core) for p in [right, left, mirror(me)] + mates + over5 + over6]
    barrier = pltpu.get_barrier_semaphore()
    for device in greet:
        pl.semaphore_signal(barrier, inc=1, device_id=device, device_id_type=MESH)

    row = lax.broadcasted_iota(jnp.int32, (B, B), 0)
    col = lax.broadcasted_iota(jnp.int32, (B, B), 1)
    perm = jnp.where(reversed_bits(row) == col, 1.0, 0.0).astype(BF)

    pl.semaphore_wait(barrier, len(greet))

    def send(src, dst, sem, device):
        copy = pltpu.make_async_remote_copy(
            src_ref=src, dst_ref=dst, send_sem=send_sem.at[sem], recv_sem=recv_sem.at[sem],
            device_id=device, device_id_type=MESH,
        )
        copy.start()
        return copy

    def arrived(ref, sem):
        pltpu.make_async_copy(ref, ref, recv_sem.at[sem]).wait()

    def gone(ref, sem):
        pltpu.make_async_copy(ref, ref, send_sem.at[sem]).wait()

    swap = send(tok_hbm, raw.at[core, pl.ds(B, rows)], 0, twin)
    to_right = send(tok_hbm.at[pl.ds(rows - B, B)], raw.at[core, pl.ds(0, B)], 1, (right, core))
    to_left = send(tok_hbm.at[pl.ds(0, B)], raw.at[core, pl.ds(rows + B, B)], 7, (left, core))

    def turn(side, b):
        tokp[side, b] = dot(perm, raw[side, b * B : (b + 1) * B]).astype(BF)

    loads[0].wait()
    for b in range(1, 5):
        turn(core, b)
    loads[1].wait()

    def split(i, carry):
        rows = pl.ds(pl.multiple_of(i * 64, 64), 64)
        pair = jnp.swapaxes(wqk[rows], 0, 1)
        wq_s[rows, :] = pair[0]
        wk_s[rows, :] = pair[1]
        return carry

    lax.fori_loop(0, wqk.shape[0] // 64, split, 0)
    loads[2].wait()

    half = pl.multiple_of(core * 512, 512)
    other = pl.multiple_of((1 - core) * 512, 512)
    weights = (wk_s, wv, wq_s)
    mine = tokp[core, 1:5].reshape(4 * B, 512)
    for i, w in enumerate(weights):
        acc[i] = dot(mine, w[pl.ds(half, 512), :])

    swap.wait()
    for b in range(1, 5):
        turn(1 - core, b)
    theirs = tokp[1 - core, 1:5].reshape(4 * B, 512)

    my_head = head_of(me)
    for i in range(3):
        full = (acc[i] + dot(theirs, weights[i][pl.ds(other, 512), :])).astype(BF)
        l1 = pool_halves(full.astype(F32), 4)
        l2 = pool_halves(l1.astype(F32), 4)
        l3 = pool_halves(l2.astype(F32), 4)
        for h in range(heads):
            cols = slice(h * HD, (h + 1) * HD)
            if i < 2:
                s3[h, i] = l3[:, cols]
                (k0, v0)[i][h, B : 5 * B] = full[:, cols]
                (k1, v1)[i][h] = l1[:, cols]
                s2[h, i] = l2[:, cols]
            else:
                sq[h] = l3[:, cols]
                q0[h] = full[:, cols]
                q1[h] = l1[:, cols]
                q2[h] = l2[:, cols]
        if i == 1:
            for p in mates:
                send(s3.at[head_of(p)], r3.at[place4], 3, (p, core))
        if i == 2:
            for p in mates:
                send(sq.at[head_of(p)], rq.at[place4], 11, (p, core))
    send(s2, r2, 2, (flip(me, 1), core))
    r3[place4] = s3[my_head]
    rq[place4] = sq[my_head]

    turned = reversed_bits(lax.broadcasted_iota(jnp.int32, (1, B), 1))
    none = jnp.zeros((1, B), F32)
    loads[3].wait()
    biases = []
    for b in range(4):
        before = (me * 4 + b - 1) * B + turned
        after = (me * 4 + b + 1) * B + turned
        biases.append(
            jnp.concatenate(
                [
                    jnp.where(before >= span[0, b], 0.0, -jnp.inf),
                    none,
                    jnp.where(after < span[1, b], 0.0, -jnp.inf),
                ],
                axis=1,
            )
        )

    def near(blocks, h, carry):
        for b in blocks:
            c = b // 2
            o = (c ^ 1) * B
            rows = slice(b * B, (b + 1) * B)
            fine = attend(q0[h, rows], k0[h, b * B : (b + 3) * B], v0[h, b * B : (b + 3) * B], biases[b])
            coarse = attend(q1[h, b * 64 : (b + 1) * 64], k1[h, o : o + B], v1[h, o : o + B])
            state = merge(fine, tuple(twice(x, 1) for x in coarse))
            fpeak[h, rows], ftot[h, rows], fnum[h, rows] = state
        return carry

    inner, outer = functools.partial(near, (1, 2)), functools.partial(near, (0, 3))
    lax.fori_loop(0, heads, inner, 0)

    to_right.wait_recv()
    relay_left = send(raw.at[core, pl.ds(0, B)], raw.at[core, pl.ds(0, B)], 8, twin)
    to_left.wait_recv()
    relay_right = send(raw.at[core, pl.ds(rows + B, B)], raw.at[core, pl.ds(rows + B, B)], 9, twin)
    arrived(r3.at[pl.ds(0, 3)], 3)
    five_rows, six_rows = pool_matrix(64, 4), pool_matrix(32, 2)
    for i in range(2):
        l4 = pool_halves(r3[:, i].astype(F32).reshape(2 * B, HD), 16)
        l5 = dot(five_rows, l4).astype(BF)
        s4[i] = l4
        s5[i] = l5
        s6[i] = dot(six_rows, l5).astype(BF)
    for p in over6:
        send(s6, r6.at[(me // 4) % 4], 6, (p, core))
    for p in over5:
        send(s5, r5.at[(me // 4) % 2], 5, (p, core))
    send(s4, r4, 4, (mirror(me), core))

    arrived(rq.at[pl.ds(0, 3)], 11)
    queries = rq[...]
    three = [
        attend(
            queries[2 * c : 2 * c + 2].reshape(B, HD),
            r3[2 - 2 * c : 4 - 2 * c, 0].reshape(B, HD),
            r3[2 - 2 * c : 4 - 2 * c, 1].reshape(B, HD),
        )
        for c in range(2)
    ]
    four = pool_halves(queries.astype(F32).reshape(2 * B, HD), 16)

    def mix(apart):
        return jnp.where((col == row) | (col == (row ^ apart)), 0.5, 0.0).astype(BF)

    five = dot(mix(4), four).astype(BF)
    six = dot(mix(2), five).astype(BF)

    relay_left.wait_recv()
    relay_right.wait_recv()
    for b in (0, 5):
        turn(core, b)
        turn(1 - core, b)

    for store, w in ((k0, wk_s), (v0, wv)):
        for b in (0, 5):
            full = dot(tokp[core, b], w[pl.ds(half, 512), :]) + dot(
                tokp[1 - core, b], w[pl.ds(other, 512), :]
            )
            full = full.astype(BF)
            for h in range(heads):
                store[h, b * B : (b + 1) * B] = full[:, h * HD : (h + 1) * HD]

    lax.fori_loop(0, NEAR_FIRST, outer, 0)

    arrived(r6, 6)
    state = attend(six, r6[:, 0].reshape(B, HD), r6[:, 1].reshape(B, HD))
    arrived(r5, 5)
    state = merge(attend(five, r5[:, 0].reshape(B, HD), r5[:, 1].reshape(B, HD)), state)
    arrived(r4, 4)
    state = merge(attend(four, r4[0], r4[1]), state)
    lines = []
    for c in range(2):
        part = tuple(twice(x[c * 64 : (c + 1) * 64], 8) for x in state)
        peak, total, numer = merge(three[c], part)
        result = numer / total
        level = peak + jnp.log2(total)
        lines.append(jnp.sum(jnp.where(row == col, level, 0.0), axis=0, keepdims=True))
        sr[2 * c, :64] = result[:64].astype(BF)
        sr[2 * c + 1, :64] = result[64:].astype(BF)
    rest = jnp.where(row[:16] < 8, lines[0], lines[1])
    stats = jnp.zeros((16, HD), F32)
    for k in range(3):
        piece = rest.astype(BF).astype(F32)
        stats = jnp.where(row[:16] % 8 == k, piece, stats)
        rest = rest - piece
    stats = stats.astype(BF)
    for j in range(4):
        sr[j, 64:] = stats
    for p in mates:
        send(sr.at[p % 4], rr.at[my_head], 10, (p, core))
    rr[my_head] = sr[place4]
    lax.fori_loop(NEAR_FIRST, heads, outer, 0)
    arrived(r2, 2)

    def second(h, carry):
        state = attend(q2[h], r2[h, 0], r2[h, 1])
        for b in range(4):
            rows = slice(b * B, (b + 1) * B)
            part = tuple(twice(twice(x[b * 32 : (b + 1) * 32], 1), 1) for x in state)
            peak, total, numer = merge((fpeak[h, rows], ftot[h, rows], fnum[h, rows]), part)
            fnum[h, rows] = numer / total
            fpeak[h, rows] = peak + jnp.log2(total)
        return carry

    lax.fori_loop(0, heads, second, 0, unroll=True)

    arrived(rr.at[pl.ds(0, 3)], 10)

    own = col[:64] == (place4 % 2) * 64 + row[:64]

    def last(h, carry):
        pieces = rr[h, 64:].astype(F32)
        line = jnp.sum(jnp.where(row[:16] // 8 == place4 // 2, pieces, 0.0), axis=0, keepdims=True)
        level = jnp.sum(jnp.where(own, line, 0.0), axis=1, keepdims=True)
        level = jnp.broadcast_to(level, (64, HD))
        cols = pl.ds(pl.multiple_of(h * HD, HD), HD)
        for b in range(4):
            rows = slice(b * B, (b + 1) * B)
            far, far_level = rr[h, b * 16 : (b + 1) * 16].astype(F32), level[b * 16 : (b + 1) * 16]
            for _ in range(3):
                far, far_level = twice(far, 1), twice(far_level, 1)
            close = fnum[h, rows]
            share = 1.0 / (1.0 + jnp.exp2(fpeak[h, rows] - far_level))
            mixed = close + (far - close) * share
            out_ref[rows, cols] = dot(perm, mixed.astype(BF)).astype(BF)
        return carry

    lax.fori_loop(0, heads, last, 0, unroll=True)

    to_right.wait_send()
    to_left.wait_send()
    relay_left.wait_send()
    relay_right.wait_send()
    gone(r2, 2)
    gone(r3.at[pl.ds(0, 3)], 3)
    gone(rq.at[pl.ds(0, 3)], 11)
    gone(r4, 4)
    gone(r5, 5)
    gone(r6, 6)
    gone(rr.at[pl.ds(0, 3)], 10)


def on_device(count, tokens, w_qk, w_value, span_start, span_end):
    rows, feats = tokens.shape
    heads = w_value.shape[1] // HD
    anywhere = pl.BlockSpec(memory_space=pltpu.HBM)

    def vm(*shape, dtype=BF):
        return pltpu.VMEM(shape, dtype)

    width = heads * HD
    scratch = [
        vm(2, rows + 2 * B, feats), vm(2, 6, B, feats), vm(2 * feats, 2, width), vm(2 * feats, width),
        vm(2 * feats, width), vm(2 * feats, width), vm(3, rows, width, dtype=F32),
        vm(heads, rows, HD), vm(heads, rows + 2 * B, HD), vm(heads, rows + 2 * B, HD),
        vm(heads, 256, HD), vm(heads, 256, HD), vm(heads, 256, HD), vm(heads, 128, HD),
        vm(heads, 2, 128, HD), vm(heads, 2, 64, HD), vm(heads, 64, HD), vm(2, 128, HD), vm(2, 64, HD), vm(2, 32, HD),
        vm(4, 80, HD),
        vm(heads, 2, 128, HD), vm(4, 2, 64, HD), vm(4, 64, HD), vm(2, 128, HD), vm(2, 2, 64, HD), vm(4, 2, 32, HD),
        vm(heads, 80, HD),
        vm(heads, rows, HD, dtype=F32), vm(heads, rows, HD, dtype=F32), vm(heads, rows, HD, dtype=F32),
        pltpu.SMEM((2, 4), jnp.int32),
        pltpu.SemaphoreType.DMA((4,)), pltpu.SemaphoreType.DMA((12,)), pltpu.SemaphoreType.DMA((12,)),
    ]
    return pl.pallas_call(
        functools.partial(kernel, count),
        out_shape=jax.ShapeDtypeStruct((rows, width), BF),
        in_specs=[anywhere] * 4,
        out_specs=pl.BlockSpec(memory_space=pltpu.VMEM),
        scratch_shapes=scratch,
        name="htransformer",
        cost_estimate=pl.CostEstimate(flops=3 * 10**9, bytes_accessed=5 * 10**6, transcendentals=10**6),
        compiler_params=pltpu.CompilerParams(
            collective_id=0, has_side_effects=True, vmem_limit_bytes=53 * 2**20
        ),
    )(tokens, w_qk, w_value, jnp.stack([span_start, span_end]))


def solution(mesh):
    placed = (P("seq", "head"), P(None, None, "head"), P(None, "head"), P("seq"), P("seq"))
    return jax.shard_map(
        functools.partial(on_device, mesh.shape["seq"]),
        mesh=mesh, in_specs=placed, out_specs=P("seq", "head"), check_vma=False,
    )
```

```python
import functools
import math

import jax
import jax.numpy as jnp
from jax import lax
from jax.experimental import pallas as pl
from jax.experimental.pallas import tpu as pltpu
from jax.sharding import PartitionSpec as P

HD = 128
B = 128
NEAR_FIRST = 2
MESH = pl.DeviceIdType.MESH
BF = jnp.bfloat16
F32 = jnp.float32
UNIT = math.log2(math.e) / math.sqrt(HD)


def reversed_bits(x, bits=7):
    out = jnp.zeros_like(x)
    for i in range(bits):
        out = out + (((x >> i) & 1) << (bits - 1 - i))
    return out


def dot(a, b):
    return jnp.dot(a, b, preferred_element_type=F32)


def pool_halves(x, blocks):
    rows, cols = x.shape
    y = x.reshape(blocks, 2, rows // (2 * blocks), cols)
    y = (y[:, 0] + y[:, 1]) * 0.5
    return y.reshape(rows // 2, cols).astype(BF)


def twice(x, blocks):
    rows, cols = x.shape
    y = x.reshape(blocks, rows // blocks, cols)
    return jnp.concatenate([y, y], axis=1).reshape(2 * rows, cols)


def attend(q, k, v, bias=None):
    s = lax.dot_general(q, k, (((1,), (1,)), ((), ())), preferred_element_type=F32)
    if bias is not None:
        s = s + bias
    top = jnp.max(s, axis=-1, keepdims=True)
    w = jnp.exp2((s - top) * UNIT).astype(BF)
    both = dot(w, jnp.concatenate([v, jnp.ones_like(v)], axis=1))
    return jnp.broadcast_to(top * UNIT, (q.shape[0], HD)), both[:, HD:], both[:, :HD]


def merge(a, b):
    top = jnp.maximum(a[0], b[0])
    ka, kb = jnp.exp2(a[0] - top), jnp.exp2(b[0] - top)
    return top, a[1] * ka + b[1] * kb, a[2] * ka + b[2] * kb


def pool_matrix(rows, run):
    r = lax.broadcasted_iota(jnp.int32, (rows, 2 * rows), 0)
    c = lax.broadcasted_iota(jnp.int32, (rows, 2 * rows), 1)
    first = (r // run) * (2 * run) + r % run
    return jnp.where((c == first) | (c == first + run), 0.5, 0.0).astype(BF)


def kernel(
    count,
    tok_hbm, wqk_hbm, wv_hbm, span_hbm,
    out_ref,
    tok_raw, tokp, wqk, wv, wq_s, wk_s, acc,
    q0, k0, v0, q1, k1, v1, q2,
    s2, s3, sq, s4, s5, s6, sr,
    r2, r3, rq, r4, r5, r6, rr,
    fpeak, ftot, fnum,
    span, load_sem, send_sem, recv_sem,
):
    me, core = lax.axis_index("seq"), lax.axis_index("head")
    heads = q0.shape[0]

    loads = [
        pltpu.make_async_copy(tok_hbm, tok_raw, load_sem.at[0]),
        pltpu.make_async_copy(wqk_hbm, wqk, load_sem.at[1]),
        pltpu.make_async_copy(wv_hbm, wv, load_sem.at[2]),
        pltpu.make_async_copy(span_hbm, span, load_sem.at[3]),
    ]
    for load in loads:
        load.start()

    def flip(device, bit):
        return device + bit * (1 - 2 * ((device // bit) % 2))

    def mirror(device):
        return device + 7 - 2 * (device % 8)

    def head_of(device):
        place = device % 4
        return place + ((device // 4) % 2) * (3 - 2 * place)

    right, left = (me + 1) % count, (me + count - 1) % count
    twin = (me, 1 - core)
    place4 = me % 4
    mates = [me - place4 + (place4 + k) % 4 for k in (1, 2, 3)]
    over5 = [flip(me, 8), mirror(flip(me, 8))]
    across = flip(me, 16)
    over6 = [across, flip(across, 8), mirror(across), mirror(flip(across, 8))]
    greet = [twin] + [(p, core) for p in [right, left, mirror(me)] + mates + over5 + over6]
    barrier = pltpu.get_barrier_semaphore()
    for device in greet:
        pl.semaphore_signal(barrier, inc=1, device_id=device, device_id_type=MESH)

    row = lax.broadcasted_iota(jnp.int32, (B, B), 0)
    col = lax.broadcasted_iota(jnp.int32, (B, B), 1)
    perm = jnp.where(reversed_bits(row) == col, 1.0, 0.0).astype(BF)

    loads[0].wait()
    for b in range(4):
        tokp[core, b + 1] = dot(perm, tok_raw[b * B : (b + 1) * B]).astype(BF)

    pl.semaphore_wait(barrier, len(greet))

    def send(src, dst, sem, device):
        copy = pltpu.make_async_remote_copy(
            src_ref=src, dst_ref=dst, send_sem=send_sem.at[sem], recv_sem=recv_sem.at[sem],
            device_id=device, device_id_type=MESH,
        )
        copy.start()
        return copy

    def arrived(ref, sem):
        pltpu.make_async_copy(ref, ref, recv_sem.at[sem]).wait()

    def gone(ref, sem):
        pltpu.make_async_copy(ref, ref, send_sem.at[sem]).wait()

    swap = send(tokp.at[core, pl.ds(1, 4)], tokp.at[core, pl.ds(1, 4)], 0, twin)
    to_right = send(tokp.at[core, 4], tokp.at[core, 0], 1, (right, core))
    to_left = send(tokp.at[core, 1], tokp.at[core, 5], 7, (left, core))

    loads[1].wait()

    def split(i, carry):
        rows = pl.ds(pl.multiple_of(i * 64, 64), 64)
        pair = jnp.swapaxes(wqk[rows], 0, 1)
        wq_s[rows, :] = pair[0]
        wk_s[rows, :] = pair[1]
        return carry

    lax.fori_loop(0, wqk.shape[0] // 64, split, 0)
    loads[2].wait()

    half = pl.multiple_of(core * 512, 512)
    other = pl.multiple_of((1 - core) * 512, 512)
    weights = (wk_s, wv, wq_s)
    mine = tokp[core, 1:5].reshape(4 * B, 512)
    for i, w in enumerate(weights):
        acc[i] = dot(mine, w[pl.ds(half, 512), :])

    swap.wait()
    theirs = tokp[1 - core, 1:5].reshape(4 * B, 512)

    my_head = head_of(me)
    for i in range(3):
        full = (acc[i] + dot(theirs, weights[i][pl.ds(other, 512), :])).astype(BF)
        l1 = pool_halves(full.astype(F32), 4)
        l2 = pool_halves(l1.astype(F32), 4)
        l3 = pool_halves(l2.astype(F32), 4)
        for h in range(heads):
            cols = slice(h * HD, (h + 1) * HD)
            if i < 2:
                s3[h, i] = l3[:, cols]
                (k0, v0)[i][h, B : 5 * B] = full[:, cols]
                (k1, v1)[i][h] = l1[:, cols]
                s2[h, i] = l2[:, cols]
            else:
                sq[h] = l3[:, cols]
                q0[h] = full[:, cols]
                q1[h] = l1[:, cols]
                q2[h] = l2[:, cols]
        if i == 1:
            for p in mates:
                send(s3.at[head_of(p)], r3.at[place4], 3, (p, core))
        if i == 2:
            for p in mates:
                send(sq.at[head_of(p)], rq.at[place4], 11, (p, core))
    send(s2, r2, 2, (flip(me, 1), core))
    r3[place4] = s3[my_head]
    rq[place4] = sq[my_head]

    turned = reversed_bits(lax.broadcasted_iota(jnp.int32, (1, B), 1))
    none = jnp.zeros((1, B), F32)
    loads[3].wait()
    biases = []
    for b in range(4):
        before = (me * 4 + b - 1) * B + turned
        after = (me * 4 + b + 1) * B + turned
        biases.append(
            jnp.concatenate(
                [
                    jnp.where(before >= span[0, b], 0.0, -jnp.inf),
                    none,
                    jnp.where(after < span[1, b], 0.0, -jnp.inf),
                ],
                axis=1,
            )
        )

    def near(blocks, h, carry):
        for b in blocks:
            c = b // 2
            o = (c ^ 1) * B
            rows = slice(b * B, (b + 1) * B)
            fine = attend(q0[h, rows], k0[h, b * B : (b + 3) * B], v0[h, b * B : (b + 3) * B], biases[b])
            coarse = attend(q1[h, b * 64 : (b + 1) * 64], k1[h, o : o + B], v1[h, o : o + B])
            state = merge(fine, tuple(twice(x, 1) for x in coarse))
            fpeak[h, rows], ftot[h, rows], fnum[h, rows] = state
        return carry

    inner, outer = functools.partial(near, (1, 2)), functools.partial(near, (0, 3))
    lax.fori_loop(0, heads, inner, 0)

    to_right.wait_recv()
    relay_left = send(tokp.at[core, 0], tokp.at[core, 0], 8, twin)
    to_left.wait_recv()
    relay_right = send(tokp.at[core, 5], tokp.at[core, 5], 9, twin)
    arrived(r3.at[pl.ds(0, 3)], 3)
    five_rows, six_rows = pool_matrix(64, 4), pool_matrix(32, 2)
    for i in range(2):
        l4 = pool_halves(r3[:, i].astype(F32).reshape(2 * B, HD), 16)
        l5 = dot(five_rows, l4).astype(BF)
        s4[i] = l4
        s5[i] = l5
        s6[i] = dot(six_rows, l5).astype(BF)
    for p in over6:
        send(s6, r6.at[(me // 4) % 4], 6, (p, core))
    for p in over5:
        send(s5, r5.at[(me // 4) % 2], 5, (p, core))
    send(s4, r4, 4, (mirror(me), core))

    arrived(rq.at[pl.ds(0, 3)], 11)
    queries = rq[...]
    three = [
        attend(
            queries[2 * c : 2 * c + 2].reshape(B, HD),
            r3[2 - 2 * c : 4 - 2 * c, 0].reshape(B, HD),
            r3[2 - 2 * c : 4 - 2 * c, 1].reshape(B, HD),
        )
        for c in range(2)
    ]
    four = pool_halves(queries.astype(F32).reshape(2 * B, HD), 16)

    def mix(apart):
        return jnp.where((col == row) | (col == (row ^ apart)), 0.5, 0.0).astype(BF)

    five = dot(mix(4), four).astype(BF)
    six = dot(mix(2), five).astype(BF)

    relay_left.wait_recv()
    relay_right.wait_recv()
    for store, w in ((k0, wk_s), (v0, wv)):
        for b in (0, 5):
            full = dot(tokp[core, b], w[pl.ds(half, 512), :]) + dot(
                tokp[1 - core, b], w[pl.ds(other, 512), :]
            )
            full = full.astype(BF)
            for h in range(heads):
                store[h, b * B : (b + 1) * B] = full[:, h * HD : (h + 1) * HD]

    lax.fori_loop(0, NEAR_FIRST, outer, 0)

    arrived(r6, 6)
    state = attend(six, r6[:, 0].reshape(B, HD), r6[:, 1].reshape(B, HD))
    arrived(r5, 5)
    state = merge(attend(five, r5[:, 0].reshape(B, HD), r5[:, 1].reshape(B, HD)), state)
    arrived(r4, 4)
    state = merge(attend(four, r4[0], r4[1]), state)
    lines = []
    for c in range(2):
        part = tuple(twice(x[c * 64 : (c + 1) * 64], 8) for x in state)
        peak, total, numer = merge(three[c], part)
        result = numer / total
        level = peak + jnp.log2(total)
        lines.append(jnp.sum(jnp.where(row == col, level, 0.0), axis=0, keepdims=True))
        sr[2 * c, :64] = result[:64].astype(BF)
        sr[2 * c + 1, :64] = result[64:].astype(BF)
    rest = jnp.where(row[:16] < 8, lines[0], lines[1])
    stats = jnp.zeros((16, HD), F32)
    for k in range(3):
        piece = rest.astype(BF).astype(F32)
        stats = jnp.where(row[:16] % 8 == k, piece, stats)
        rest = rest - piece
    stats = stats.astype(BF)
    for j in range(4):
        sr[j, 64:] = stats
    for p in mates:
        send(sr.at[p % 4], rr.at[my_head], 10, (p, core))
    rr[my_head] = sr[place4]
    lax.fori_loop(NEAR_FIRST, heads, outer, 0)
    arrived(r2, 2)

    def second(h, carry):
        state = attend(q2[h], r2[h, 0], r2[h, 1])
        for b in range(4):
            rows = slice(b * B, (b + 1) * B)
            part = tuple(twice(twice(x[b * 32 : (b + 1) * 32], 1), 1) for x in state)
            peak, total, numer = merge((fpeak[h, rows], ftot[h, rows], fnum[h, rows]), part)
            fnum[h, rows] = numer / total
            fpeak[h, rows] = peak + jnp.log2(total)
        return carry

    lax.fori_loop(0, heads, second, 0, unroll=True)

    arrived(rr.at[pl.ds(0, 3)], 10)

    own = col[:64] == (place4 % 2) * 64 + row[:64]

    def last(h, carry):
        pieces = rr[h, 64:].astype(F32)
        line = jnp.sum(jnp.where(row[:16] // 8 == place4 // 2, pieces, 0.0), axis=0, keepdims=True)
        level = jnp.sum(jnp.where(own, line, 0.0), axis=1, keepdims=True)
        level = jnp.broadcast_to(level, (64, HD))
        cols = pl.ds(pl.multiple_of(h * HD, HD), HD)
        for b in range(4):
            rows = slice(b * B, (b + 1) * B)
            far, far_level = rr[h, b * 16 : (b + 1) * 16].astype(F32), level[b * 16 : (b + 1) * 16]
            for _ in range(3):
                far, far_level = twice(far, 1), twice(far_level, 1)
            close = fnum[h, rows]
            share = 1.0 / (1.0 + jnp.exp2(fpeak[h, rows] - far_level))
            mixed = close + (far - close) * share
            out_ref[rows, cols] = dot(perm, mixed.astype(BF)).astype(BF)
        return carry

    lax.fori_loop(0, heads, last, 0, unroll=True)

    to_right.wait_send()
    to_left.wait_send()
    relay_left.wait_send()
    relay_right.wait_send()
    gone(r2, 2)
    gone(r3.at[pl.ds(0, 3)], 3)
    gone(rq.at[pl.ds(0, 3)], 11)
    gone(r4, 4)
    gone(r5, 5)
    gone(r6, 6)
    gone(rr.at[pl.ds(0, 3)], 10)


def on_device(count, tokens, w_qk, w_value, span_start, span_end):
    rows, feats = tokens.shape
    heads = w_value.shape[1] // HD
    anywhere = pl.BlockSpec(memory_space=pltpu.HBM)

    def vm(*shape, dtype=BF):
        return pltpu.VMEM(shape, dtype)

    width = heads * HD
    scratch = [
        vm(rows, feats), vm(2, 6, B, feats), vm(2 * feats, 2, width), vm(2 * feats, width),
        vm(2 * feats, width), vm(2 * feats, width), vm(3, rows, width, dtype=F32),
        vm(heads, rows, HD), vm(heads, rows + 2 * B, HD), vm(heads, rows + 2 * B, HD),
        vm(heads, 256, HD), vm(heads, 256, HD), vm(heads, 256, HD), vm(heads, 128, HD),
        vm(heads, 2, 128, HD), vm(heads, 2, 64, HD), vm(heads, 64, HD), vm(2, 128, HD), vm(2, 64, HD), vm(2, 32, HD),
        vm(4, 80, HD),
        vm(heads, 2, 128, HD), vm(4, 2, 64, HD), vm(4, 64, HD), vm(2, 128, HD), vm(2, 2, 64, HD), vm(4, 2, 32, HD),
        vm(heads, 80, HD),
        vm(heads, rows, HD, dtype=F32), vm(heads, rows, HD, dtype=F32), vm(heads, rows, HD, dtype=F32),
        pltpu.SMEM((2, 4), jnp.int32),
        pltpu.SemaphoreType.DMA((4,)), pltpu.SemaphoreType.DMA((12,)), pltpu.SemaphoreType.DMA((12,)),
    ]
    return pl.pallas_call(
        functools.partial(kernel, count),
        out_shape=jax.ShapeDtypeStruct((rows, width), BF),
        in_specs=[anywhere] * 4,
        out_specs=pl.BlockSpec(memory_space=pltpu.VMEM),
        scratch_shapes=scratch,
        name="htransformer",
        cost_estimate=pl.CostEstimate(flops=3 * 10**9, bytes_accessed=5 * 10**6, transcendentals=10**6),
        compiler_params=pltpu.CompilerParams(
            collective_id=0, has_side_effects=True, vmem_limit_bytes=53 * 2**20
        ),
    )(tokens, w_qk, w_value, jnp.stack([span_start, span_end]))


def solution(mesh):
    placed = (P("seq", "head"), P(None, None, "head"), P(None, "head"), P("seq"), P("seq"))
    return jax.shard_map(
        functools.partial(on_device, mesh.shape["seq"]),
        mesh=mesh, in_specs=placed, out_specs=P("seq", "head"), check_vma=False,
    )
```
